256 devices in a mesh: dp: 4 (over y_lo, core), seq: 32 (over z, x), tensor: 2 (over y_hi).
Axes of the slice: x: 4, y: 4 (y_hi: 2, y_lo: 2; y = y_hi * 2 + y_lo), z: 8, core: 2. Of those that a mesh axis runs over, the one named last changes fastest.
Arguments:
- lengths: int32 [4], P('dp'), may hold values from 3072 to 12288, as said below
- query_act: bfloat16 [4, 12288, 1024], P('dp', 'seq', 'tensor'), may hold values from -6 to 6
- key_act: bfloat16 [4, 12288, 1024], P('dp', 'seq', 'tensor'), may hold values from -6 to 6
- value_act: bfloat16 [4, 12288, 1024], P('dp', 'seq', 'tensor'), may hold values from -6 to 6
- conv_input: bfloat16 [4, 12288, 1024], P('dp', 'seq'), may hold values from -6 to 6
- conv_result: bfloat16 [4, 12288, 1024], P('dp', 'seq', 'tensor'), may hold values from -6 to 6
- out_grad: bfloat16 [4, 12288, 1024], P('dp', 'seq'), may hold values from -6 to 6
- out_weight: bfloat16 [1024, 1024], P('tensor'), may hold values from -0.1875 to 0.1875
- glu_weight: bfloat16 [2, 1024, 1024], P(None, None, 'tensor'), may hold values from -0.1875 to 0.1875
- conv_taps: bfloat16 [31, 1024], P(None, 'tensor'), may hold values from -1 to 1
- proj_weight: bfloat16 [1024, 1024], P('tensor'), may hold values from -0.1875 to 0.1875
Outputs:
- input_grad: bfloat16 [4, 12288, 1024], P('dp', 'seq')
- query_grad: bfloat16 [4, 12288, 1024], P('dp', 'seq', 'tensor')
- key_grad: bfloat16 [4, 12288, 1024], P('dp', 'seq', 'tensor')
- value_grad: bfloat16 [4, 12288, 1024], P('dp', 'seq', 'tensor')
- out_weight_grad: bfloat16 [1024, 1024], P('tensor', ('dp', 'seq'))
- glu_weight_grad: bfloat16 [2, 1024, 1024], P(None, ('dp', 'seq'), 'tensor')
- proj_weight_grad: bfloat16 [1024, 1024], P('tensor', ('dp', 'seq'))
The draws below stay inside these ranges and needn't reach their ends.
Inputs may be any that keep to these rules, and one draw needn't show every extreme that they name: `lengths`: every length is at least 3072, and in every draw one recording has all 12288 frames valid.
All inputs are finite; a program needn't handle non-finite values.
Results may differ from the reference program's by a relative error of at most 0.013.
Values may be sent and summed in bfloat16 or wider, within the bound.
No kernel may reach another device: no remote copies, remote signals or barrier semaphores. Data moves between devices by JAX's collectives and lax.ppermute only.
A program may use at most 128 MiB of HBM per device.

```python
import jax
import jax.numpy as jnp
from jax import lax

D = 1024
HEADS = 16
HEAD_DIM = 64
KERNEL = 31
WIN = 256
TOK_DEV = 384
FRAMES = 12288
RECS = 4


def draw_lengths(key, part):
    key = jax.random.fold_in(key, 11)
    first_key, second_key = jax.random.split(key)
    drawn = jax.random.randint(first_key, (RECS,), FRAMES // 4, FRAMES + 1)
    full_index = jax.random.randint(second_key, (), 0, RECS)
    return jnp.where(jnp.arange(RECS) == full_index, FRAMES, drawn).astype(jnp.int32)


def draw_query_act(key, part):
    key = jax.random.fold_in(key, 21)
    shape = (RECS, FRAMES, HEADS * HEAD_DIM)
    return jnp.clip(jax.random.normal(key, shape, jnp.float32), -6.0, 6.0).astype(jnp.bfloat16)


def draw_key_act(key, part):
    key = jax.random.fold_in(key, 31)
    shape = (RECS, FRAMES, HEADS * HEAD_DIM)
    return jnp.clip(jax.random.normal(key, shape, jnp.float32), -6.0, 6.0).astype(jnp.bfloat16)


def with_spikes(values, stream_key, source, target, parts, factor):
    def block_of(axis_at):
        return (jnp.arange(values.shape[axis_at]) // (values.shape[axis_at] // parts)).reshape((-1,) + (1,) * (values.ndim - 1 - axis_at))

    first = jax.random.permutation(stream_key, parts)[block_of(target)]
    far = (block_of(target) + parts // 2) % parts
    return jnp.where((block_of(source) == first) | (block_of(source) == far), factor * values, values)


def shard_levels(rng, extent, cuts, low, high):
    def one(dim, shards_of):
        draws = jax.random.uniform(jax.random.fold_in(jax.random.fold_in(rng, 6), dim), (shards_of,), jnp.float32, low / len(cuts), high / len(cuts))
        return jnp.repeat(jnp.exp(draws), extent[dim] // shards_of).reshape((-1,) + (1,) * (len(extent) - dim - 1))

    level = one(*cuts[0])
    for cut in cuts[1:]:
        level = level * one(*cut)
    return level


def scatter_about(key, dims, spread, reach, cuts=(), kind=jnp.bfloat16):
    gain = shard_levels(key, dims, cuts, -0.22, 0.18) if cuts else 1.0
    entries = jax.random.normal(key, dims, jnp.float32) * spread * gain
    return jnp.minimum(jnp.maximum(entries, -reach), reach).astype(kind)


def noise_with(stream_key, extent, scale, most, cuts, heavy, kind=jnp.bfloat16):
    result = scale * jax.random.normal(stream_key, extent, jnp.float32)
    if cuts:
        result = result * shard_levels(stream_key, extent, cuts, -0.22, 0.18)
    return jnp.clip(with_spikes(result, jax.random.fold_in(stream_key, 3), *heavy), -most, most).astype(kind)


def setup_inputs(seed: int = 0) -> dict:
    streams_of = jax.random.split(jax.random.key(seed), 12)
    return {
        "lengths": draw_lengths(jax.random.fold_in(streams_of[11], 71), 0),
        "query_act": draw_query_act(jax.random.fold_in(streams_of[11], 71), 0),
        "key_act": draw_key_act(jax.random.fold_in(streams_of[11], 71), 0),
        "value_act": scatter_about(streams_of[3], (RECS, FRAMES, HEADS * HEAD_DIM), 1.0, 6.0, ((0, 4), (1, 32), (2, 2))),
        "conv_input": scatter_about(streams_of[4], (RECS, FRAMES, D), 1.0, 6.0, ((0, 4), (1, 32))),
        "conv_result": scatter_about(streams_of[5], (RECS, FRAMES, D), 1.0, 6.0, ((0, 4), (1, 32), (2, 2))),
        "out_grad": noise_with(streams_of[6], (RECS, FRAMES, D), 1.0, 6.0, ((0, 4), (1, 32)), (1, 2, 32, 2.75)),
        "out_weight": scatter_about(streams_of[7], (HEADS * HEAD_DIM, D), (HEADS * HEAD_DIM) ** -0.5, 0.1875, ((0, 2),)),
        "glu_weight": scatter_about(streams_of[8], (2, D, D), D ** -0.5, 0.1875, ((2, 2),)),
        "conv_taps": scatter_about(streams_of[9], (KERNEL, D), KERNEL ** -0.5, 1.0, ((1, 2),)),
        "proj_weight": scatter_about(streams_of[10], (D, D), D ** -0.5, 0.1875, ((0, 2),)),
    }


NEG_FILL = -1e30


def silu_slope(pre_act):
    logistic = jax.nn.sigmoid(pre_act)
    return logistic * (1.0 + pre_act * (1.0 - logistic))


def tap_sum(padded, conv_taps, frames):
    kernel = conv_taps.shape[0]
    summed = jnp.zeros((frames, padded.shape[1]), jnp.float32)
    for offset in range(kernel):
        start_row = kernel - 1 - offset
        summed = summed + conv_taps[offset].astype(jnp.float32) * padded[start_row:start_row + frames].astype(jnp.float32)
    return summed


def head_grads(operands, q_pos, k_pos, length, query_mask):
    q_head, k_head, v_head, d_head = operands
    score_scale = q_head.shape[1] ** -0.5
    allowed = (jnp.abs(q_pos[:, None] - k_pos[None, :]) <= WIN) & (k_pos[None, :] >= 0) & (k_pos[None, :] < length)
    scores = jnp.dot(q_head, k_head.T, preferred_element_type=jnp.float32) * score_scale
    scores = jnp.where(allowed, scores, NEG_FILL)
    row_top = jnp.max(scores, axis=1, keepdims=True)
    exponent = jnp.exp(scores - row_top)
    attn_prob = exponent / jnp.sum(exponent, axis=1, keepdims=True)
    prob_low = attn_prob.astype(jnp.bfloat16)
    attended = jnp.dot(prob_low, v_head, preferred_element_type=jnp.float32) * query_mask[:, None]
    grad_prob = jnp.dot(d_head, v_head.T, preferred_element_type=jnp.float32)
    row_delta = jnp.sum(attn_prob * grad_prob, axis=1, keepdims=True)
    grad_score = (attn_prob * (grad_prob - row_delta) * score_scale).astype(jnp.bfloat16)
    grad_query = jnp.dot(grad_score, k_head, preferred_element_type=jnp.float32).astype(jnp.bfloat16)
    grad_key = jnp.dot(grad_score.T, q_head, preferred_element_type=jnp.float32)
    grad_value = jnp.dot(prob_low.T, d_head, preferred_element_type=jnp.float32)
    return grad_query, grad_key, grad_value, attended.astype(jnp.bfloat16)


def attend(q_rows, kv_rows, d_rows, q_pos, k_pos, length):
    frames, head_cols = q_rows.shape
    key_span = kv_rows.shape[0]
    heads = head_cols // HEAD_DIM
    query_mask = (q_pos < length).astype(jnp.float32)

    def split_heads(values, rows):
        return values.reshape(rows, heads, HEAD_DIM).transpose(1, 0, 2)

    def one_head(operands):
        return head_grads(operands, q_pos, k_pos, length, query_mask)

    results = lax.map(one_head, (split_heads(q_rows, frames), split_heads(kv_rows[:, :head_cols], key_span), split_heads(kv_rows[:, head_cols:], key_span), split_heads(d_rows, frames)))

    def join_heads(values):
        return values.transpose(1, 0, 2).reshape(values.shape[1], head_cols)

    grad_query, grad_key, grad_value, attended = [join_heads(stacked) for stacked in results]
    return grad_query, jnp.concatenate([grad_key, grad_value], axis=1), attended


def reference(lengths, query_act, key_act, value_act, conv_input, conv_result, out_grad, out_weight, glu_weight, conv_taps, proj_weight):
    def one_recording(operands):
        length, q_rows, k_rows, v_rows, resid_rows, pre_rows, out_rows = operands
        frames, head_cols = q_rows.shape
        positions = jnp.arange(frames, dtype=jnp.int32)
        frame_mask = (positions < length).astype(jnp.float32)
        pre_float = pre_rows.astype(jnp.float32)
        activated = jax.nn.silu(pre_float).astype(jnp.bfloat16)
        grad_act = jnp.dot(out_rows, proj_weight.T, preferred_element_type=jnp.float32)
        grad_pre = (grad_act * silu_slope(pre_float)).astype(jnp.bfloat16)
        half_width = (conv_taps.shape[0] - 1) // 2
        padded = jnp.pad(grad_pre, ((half_width, half_width), (0, 0)))
        grad_conv = tap_sum(padded, conv_taps, frames) * frame_mask[:, None]
        value_half = jnp.dot(resid_rows, glu_weight[0], preferred_element_type=jnp.float32)
        gate_half = jnp.dot(resid_rows, glu_weight[1], preferred_element_type=jnp.float32)
        logistic = jax.nn.sigmoid(gate_half)
        grad_glu = jnp.stack([grad_conv * logistic, grad_conv * value_half * logistic * (1.0 - logistic)]).astype(jnp.bfloat16)
        grad_resid = out_rows.astype(jnp.float32) + jnp.dot(grad_glu[0], glu_weight[0].T, preferred_element_type=jnp.float32) + jnp.dot(grad_glu[1], glu_weight[1].T, preferred_element_type=jnp.float32)
        resid_low = grad_resid.astype(jnp.bfloat16)
        glu_term = jnp.einsum("fd,hfc->hdc", resid_rows.astype(jnp.float32), grad_glu.astype(jnp.float32))
        proj_term = jnp.dot(activated.T, out_rows, preferred_element_type=jnp.float32)
        grad_attn = (jnp.dot(resid_low, out_weight.T, preferred_element_type=jnp.float32) * frame_mask[:, None]).astype(jnp.bfloat16)
        kv_padded = jnp.pad(jnp.concatenate([k_rows, v_rows], axis=1), ((WIN, WIN), (0, 0)))
        key_span = TOK_DEV + 2 * WIN

        def block_step(state_pair, block_index):
            returned, out_term = state_pair
            start_row = block_index * TOK_DEV
            q_pos = start_row + jnp.arange(TOK_DEV, dtype=jnp.int32)
            k_pos = start_row - WIN + jnp.arange(key_span, dtype=jnp.int32)
            grad_query, grad_kv, attended = attend(
                lax.dynamic_slice_in_dim(q_rows, start_row, TOK_DEV, 0),
                lax.dynamic_slice_in_dim(kv_padded, start_row, key_span, 0),
                lax.dynamic_slice_in_dim(grad_attn, start_row, TOK_DEV, 0),
                q_pos, k_pos, length)
            current = lax.dynamic_slice_in_dim(returned, start_row, key_span, 0)
            returned = lax.dynamic_update_slice_in_dim(returned, current + grad_kv, start_row, 0)
            resid_block = lax.dynamic_slice_in_dim(resid_low, start_row, TOK_DEV, 0)
            out_term = out_term + jnp.dot(attended.T, resid_block, preferred_element_type=jnp.float32)
            return (returned, out_term), grad_query

        initial = (jnp.zeros((frames + 2 * WIN, 2 * head_cols), jnp.float32), jnp.zeros((head_cols, resid_rows.shape[1]), jnp.float32))
        (returned, out_term), grad_blocks = lax.scan(block_step, initial, jnp.arange(frames // TOK_DEV, dtype=jnp.int32))
        grad_kv = returned[WIN:WIN + frames]
        outputs = (resid_low, grad_blocks.reshape(frames, head_cols), grad_kv[:, :head_cols].astype(jnp.bfloat16), grad_kv[:, head_cols:].astype(jnp.bfloat16))
        return outputs, (out_term, glu_term, proj_term)

    recorded, weight_terms = lax.map(one_recording, (lengths, query_act, key_act, value_act, conv_input, conv_result, out_grad))
    return (recorded[0], recorded[1], recorded[2], recorded[3],
            jnp.sum(weight_terms[0], axis=0).astype(jnp.bfloat16),
            jnp.sum(weight_terms[1], axis=0).astype(jnp.bfloat16),
            jnp.sum(weight_terms[2], axis=0).astype(jnp.bfloat16))
```

```python
import jax
import jax.numpy as jnp
from jax import lax
from jax.sharding import PartitionSpec as P

HEAD_DIM = 64
WIN = 256


NEG_FILL = -1e30


def extended(shard, sides, width):
    for axis, dim in sides:
        peers, length = (lax.axis_size(axis), shard.shape[dim])
        up = [(i, (i + 1) % peers) for i in range(peers - 1)]
        down = [(j, i) for i, j in up]
        last = lax.slice_in_dim(shard, length - width, length, axis=dim)
        leading = lax.slice_in_dim(shard, 0, width, axis=dim)
        before = lax.ppermute(last, axis, up)
        after = lax.ppermute(leading, axis, down)
        shard = jnp.concatenate([before, shard, after], axis=dim)
    return shard


def from_behind(value, axis, steps):
    count = lax.axis_size(axis)
    leading, last = (max(0, -steps), min(count, count - steps))
    return lax.ppermute(value, axis, [(source, source + steps) for source in range(leading, last)])


def silu_slope(pre_act):
    logistic = jax.nn.sigmoid(pre_act)
    return logistic * (1.0 + pre_act * (1.0 - logistic))


def tap_sum(padded, conv_taps, frames):
    kernel = conv_taps.shape[0]
    summed = jnp.zeros((frames, padded.shape[1]), jnp.float32)
    for offset in range(kernel):
        start_row = kernel - 1 - offset
        summed = summed + conv_taps[offset].astype(jnp.float32) * padded[
            start_row : start_row + frames
        ].astype(jnp.float32)
    return summed


def head_grads(operands, q_pos, k_pos, length, query_mask):
    q_head, k_head, v_head, d_head = operands
    score_scale = q_head.shape[1] ** (-0.5)
    allowed = (
        (jnp.abs(q_pos[:, None] - k_pos[None, :]) <= WIN)
        & (k_pos[None, :] >= 0)
        & (k_pos[None, :] < length)
    )
    scores = jnp.dot(q_head, k_head.T, preferred_element_type=jnp.float32) * score_scale
    scores = jnp.where(allowed, scores, NEG_FILL)
    row_top = jnp.max(scores, axis=1, keepdims=True)
    exponent = jnp.exp(scores - row_top)
    attn_prob = exponent / jnp.sum(exponent, axis=1, keepdims=True)
    prob_low = attn_prob.astype(jnp.bfloat16)
    attended = jnp.dot(prob_low, v_head, preferred_element_type=jnp.float32) * query_mask[:, None]
    grad_prob = jnp.dot(d_head, v_head.T, preferred_element_type=jnp.float32)
    row_delta = jnp.sum(attn_prob * grad_prob, axis=1, keepdims=True)
    grad_score = (attn_prob * (grad_prob - row_delta) * score_scale).astype(jnp.bfloat16)
    grad_query = jnp.dot(grad_score, k_head, preferred_element_type=jnp.float32).astype(
        jnp.bfloat16
    )
    grad_key = jnp.dot(grad_score.T, q_head, preferred_element_type=jnp.float32)
    grad_value = jnp.dot(prob_low.T, d_head, preferred_element_type=jnp.float32)
    return (grad_query, grad_key, grad_value, attended.astype(jnp.bfloat16))


def attend(q_rows, kv_rows, d_rows, q_pos, k_pos, length):
    frames, head_cols = q_rows.shape
    key_span = kv_rows.shape[0]
    heads = head_cols // HEAD_DIM
    query_mask = (q_pos < length).astype(jnp.float32)

    def split_heads(values, rows):
        return values.reshape(rows, heads, HEAD_DIM).transpose(1, 0, 2)

    def one_head(operands):
        return head_grads(operands, q_pos, k_pos, length, query_mask)

    results = lax.map(
        one_head,
        (
            split_heads(q_rows, frames),
            split_heads(kv_rows[:, :head_cols], key_span),
            split_heads(kv_rows[:, head_cols:], key_span),
            split_heads(d_rows, frames),
        ),
    )

    def join_heads(values):
        return values.transpose(1, 0, 2).reshape(values.shape[1], head_cols)

    grad_query, grad_key, grad_value, attended = [join_heads(stacked) for stacked in results]
    return (grad_query, jnp.concatenate([grad_key, grad_value], axis=1), attended)


def swapped(value, axis, stride):
    count = lax.axis_size(axis)
    return lax.ppermute(value, axis, [(i, i ^ stride) for i in range(count)])


def halved(value, bit, axis, stride):
    half = value.shape[0] // 2
    mine = lax.dynamic_slice_in_dim(value, bit * half, half, axis=0)
    other = lax.dynamic_slice_in_dim(value, (1 - bit) * half, half, axis=0)
    arrived = swapped(other.astype(jnp.bfloat16), axis, stride)
    return (mine.astype(jnp.float32) + arrived.astype(jnp.float32)).astype(jnp.bfloat16)


def reduce_weights(terms):
    place = lax.axis_index("dp")
    core, y_lo = (place % 2, place // 2)
    rows, cols = terms.shape
    by_core = terms.reshape(2, 2, rows // 4, cols).transpose(1, 0, 2, 3)
    on_chip = halved(by_core, core, "dp", 1)[0]
    on_pair = halved(on_chip, y_lo, "dp", 2)[0]
    peers = lax.axis_size("seq")
    arrived = lax.all_to_all(on_pair.reshape(peers, rows // 4 // peers, cols), "seq", 0, 0)
    return jnp.sum(arrived.astype(jnp.float32), axis=0)


def local(
    lengths,
    query_act,
    key_act,
    value_act,
    conv_input,
    conv_result,
    out_grad,
    out_weight,
    glu_weight,
    conv_taps,
    proj_weight,
):
    length = lengths[0]
    q_rows = query_act[0]
    frames, head_cols = q_rows.shape
    first_frame = lax.axis_index("seq") * frames
    positions = first_frame + jnp.arange(frames, dtype=jnp.int32)
    frame_mask = (positions < length).astype(jnp.float32)
    kv_ext = extended(jnp.concatenate([key_act[0], value_act[0]], axis=1), (("seq", 0),), WIN)
    resid_rows = conv_input[0]
    out_rows = out_grad[0]
    pre_float = conv_result[0].astype(jnp.float32)
    activated = jax.nn.silu(pre_float).astype(jnp.bfloat16)
    grad_act = jnp.dot(out_rows, proj_weight.T, preferred_element_type=jnp.float32)
    grad_pre = (grad_act * silu_slope(pre_float)).astype(jnp.bfloat16)
    half_width = (conv_taps.shape[0] - 1) // 2
    padded = extended(grad_pre, (("seq", 0),), half_width)
    grad_conv = tap_sum(padded, conv_taps, frames) * frame_mask[:, None]
    value_half = jnp.dot(resid_rows, glu_weight[0], preferred_element_type=jnp.float32)
    gate_half = jnp.dot(resid_rows, glu_weight[1], preferred_element_type=jnp.float32)
    logistic = jax.nn.sigmoid(gate_half)
    grad_glu = jnp.stack(
        [grad_conv * logistic, grad_conv * value_half * logistic * (1.0 - logistic)]
    ).astype(jnp.bfloat16)
    local_cols = grad_glu.shape[2]
    partial_grad = lax.dot_general(
        grad_glu, glu_weight, (((0, 2), (0, 2)), ((), ())), preferred_element_type=jnp.float32
    )
    glu_rows = jnp.einsum(
        "fd,hfc->dhc", resid_rows, grad_glu, preferred_element_type=jnp.float32
    ).reshape(resid_rows.shape[1], 2 * local_cols)
    proj_term = jnp.dot(out_rows.T, activated, preferred_element_type=jnp.float32)
    own_grad = partial_grad.astype(jnp.bfloat16)
    other_grad = swapped(own_grad, "tensor", 1)
    channel_sum = own_grad.astype(jnp.float32) + other_grad.astype(jnp.float32)
    grad_resid = out_rows.astype(jnp.float32) + channel_sum
    resid_low = grad_resid.astype(jnp.bfloat16)
    grad_attn = (
        jnp.dot(resid_low, out_weight.T, preferred_element_type=jnp.float32) * frame_mask[:, None]
    ).astype(jnp.bfloat16)
    key_span = kv_ext.shape[0]
    k_pos = first_frame - WIN + jnp.arange(key_span, dtype=jnp.int32)
    operands = (q_rows, kv_ext, grad_attn)
    grad_query, grad_kv, attended = attend(
        operands[0], operands[1], operands[2], positions, k_pos, length
    )
    summed = grad_kv[WIN : WIN + frames]
    tail_rows = frames - WIN
    for offset, edge_rows in ((-1, grad_kv[:WIN]), (1, grad_kv[WIN + frames :])):
        arrived = from_behind(edge_rows.astype(jnp.bfloat16), "seq", offset).astype(edge_rows.dtype)
        if offset < 0:
            summed = summed + jnp.pad(arrived, ((tail_rows, 0), (0, 0)))
        else:
            summed = summed + jnp.pad(arrived, ((0, tail_rows), (0, 0)))
    out_term = jnp.dot(resid_low.T, attended, preferred_element_type=jnp.float32)
    joined = reduce_weights(jnp.concatenate([out_term, glu_rows, proj_term], axis=1))
    out_sum = joined[:, :head_cols].T
    glu_sum = joined[:, head_cols : 3 * head_cols].reshape(-1, 2, local_cols).transpose(1, 0, 2)
    proj_sum = joined[:, 3 * head_cols :].T
    return (
        resid_low[None],
        grad_query[None],
        summed[:, :head_cols].astype(jnp.bfloat16)[None],
        summed[:, head_cols:].astype(jnp.bfloat16)[None],
        out_sum.astype(jnp.bfloat16),
        glu_sum.astype(jnp.bfloat16),
        proj_sum.astype(jnp.bfloat16),
    )


def solution(mesh):
    in_specs = (
        P("dp"),
        P("dp", "seq", "tensor"),
        P("dp", "seq", "tensor"),
        P("dp", "seq", "tensor"),
        P("dp", "seq", None),
        P("dp", "seq", "tensor"),
        P("dp", "seq", None),
        P("tensor", None),
        P(None, None, "tensor"),
        P(None, "tensor"),
        P("tensor", None),
    )
    out_specs = (
        P("dp", "seq", None),
        P("dp", "seq", "tensor"),
        P("dp", "seq", "tensor"),
        P("dp", "seq", "tensor"),
        P("tensor", ("dp", "seq")),
        P(None, ("dp", "seq"), "tensor"),
        P("tensor", ("dp", "seq")),
    )
    return jax.shard_map(local, mesh=mesh, in_specs=in_specs, out_specs=out_specs, check_vma=False)
```

```python
import functools

import jax
import jax.numpy as jnp
from jax import lax
from jax.experimental import pallas as pl
from jax.experimental.pallas import tpu as pltpu
from jax.sharding import PartitionSpec as P

HEAD_DIM = 64
WIN = 256


NEG_FILL = -1e30
FULL, LOW = jnp.float32, jnp.bfloat16
TAPS = 31
EDGE = 16
STRIP = 32
VMEM = pl.BlockSpec(memory_space=pltpu.VMEM)
SMEM = pl.BlockSpec(memory_space=pltpu.SMEM)


def shape(dims, kind=LOW):
    return jax.ShapeDtypeStruct(dims, kind)


def call(kernel, name, operands, in_specs, out_shape, out_specs=None, scratch=(), flops=0, moved=0, limit=24, **more):
    return pl.pallas_call(
        kernel,
        in_specs=in_specs,
        out_specs=[VMEM] * len(out_shape) if out_specs is None else out_specs,
        out_shape=out_shape,
        scratch_shapes=list(scratch),
        compiler_params=pltpu.CompilerParams(vmem_limit_bytes=limit * 2**20),
        cost_estimate=pl.CostEstimate(flops=flops, bytes_accessed=moved, transcendentals=0),
        name=name,
        **more,
    )(*operands)


def dot_nt(left, right):
    return lax.dot_general(left, right, (((1,), (1,)), ((), ())), preferred_element_type=FULL)


def dot_tn(left, right):
    return lax.dot_general(left, right, (((0,), (0,)), ((), ())), preferred_element_type=FULL)


def round_ring(value, steps):
    count = lax.axis_size("seq")
    return lax.ppermute(value, "seq", [(i, (i + steps) % count) for i in range(count)])


def swapped(value, axis, stride):
    count = lax.axis_size(axis)
    return lax.ppermute(value, axis, [(i, i ^ stride) for i in range(count)])


def pack_kernel(k_ref, v_ref, grad_ref, pre_ref, up_ref, down_ref):
    frames, cols = k_ref.shape
    for out_ref, start, edge in ((up_ref, frames - WIN, frames - EDGE), (down_ref, 0, 0)):
        out_ref[:WIN, :cols] = k_ref[start : start + WIN]
        out_ref[:WIN, cols:] = v_ref[start : start + WIN]
        out_ref[WIN : WIN + EDGE] = grad_ref[edge : edge + EDGE]
        out_ref[WIN + EDGE :, :cols] = pre_ref[edge : edge + EDGE]
        out_ref[WIN + EDGE :, cols:] = pre_ref[edge : edge + EDGE]


def pack(k_rows, v_rows, out_rows, pre_rows):
    dims = (WIN + 2 * EDGE, 2 * k_rows.shape[1])
    return call(pack_kernel, "pack", (k_rows, v_rows, out_rows, pre_rows), [VMEM] * 4, [shape(dims)] * 2, moved=2**21)


def pre_grad(out_rows, pre_rows, proj):
    pre = pre_rows.astype(FULL)
    logistic = jax.nn.sigmoid(pre)
    slope = logistic * (1.0 + pre * (1.0 - logistic))
    return (dot_nt(out_rows, proj) * slope).astype(LOW), (pre * logistic).astype(LOW)


def conv_strip(rows, taps):
    count = rows.shape[0] - 2 * EDGE
    total = jnp.zeros((count, rows.shape[1]), FULL)
    for shift in range(8):
        moved = rows[shift : shift + count + 24]
        for coarse in range(4):
            step = 8 * coarse + shift
            if step >= 1:
                total = total + taps[TAPS - step : TAPS - step + 1] * moved[8 * coarse : 8 * coarse + count]
    return total


def glu_grads(grad_conv, logistic, value):
    first = grad_conv * logistic
    return first.astype(LOW), (first * value * (1.0 - logistic)).astype(LOW)


def front_kernel(
    place, out_ref, pre_ref, proj_ref, input_ref, glu_w_ref, taps_ref,
    mid_ref, glu_ref, act_ref, rim_ref, rim_gate_ref, rim_value_ref,
    padded, taps, gates, values,
):
    frames, cols = pre_ref.shape
    first, length = place[0], place[1]
    inner = frames - EDGE
    taps[:TAPS] = taps_ref[...].astype(FULL)
    for part in range(0, cols, 256):
        span = slice(part, part + 256)
        grad_pre, activated = pre_grad(out_ref[...], pre_ref[:, span], proj_ref[span])
        act_ref[:, span] = activated
        padded[:, span] = grad_pre.astype(FULL)
        rim_ref[: 2 * EDGE, span] = grad_pre[: 2 * EDGE]
        rim_ref[2 * EDGE :, span] = grad_pre[frames - 2 * EDGE :]
        values[:, span] = jnp.dot(input_ref[...], glu_w_ref[0, :, span], preferred_element_type=FULL)
        gate_half = jnp.dot(input_ref[...], glu_w_ref[1, :, span], preferred_element_type=FULL)
        gates[:, span] = jax.nn.sigmoid(gate_half)
    for whole, rim in ((gates, rim_gate_ref), (values, rim_value_ref)):
        rim[:EDGE] = whole[:EDGE]
        rim[EDGE:] = whole[inner:]

    def strip(i, carry):
        at = pl.multiple_of(i * STRIP, STRIP)
        rows = pl.ds(pl.multiple_of(at + EDGE, EDGE), STRIP)
        frame = lax.broadcasted_iota(jnp.int32, (STRIP, 128), 0) + (first + EDGE + at)
        valid = frame < length
        for part in range(0, cols, 128):
            span = slice(part, part + 128)
            grad_conv = conv_strip(padded[pl.ds(at, STRIP + 2 * EDGE), span], taps[:, span])
            grad_conv = jnp.where(valid, grad_conv, 0.0)
            low = glu_grads(grad_conv, gates[rows, span], values[rows, span])
            glu_ref[rows, span] = low[0]
            glu_ref[rows, cols + part : cols + part + 128] = low[1]
        return carry

    lax.fori_loop(0, (frames - 2 * EDGE) // STRIP, strip, 0)
    for part in range(0, mid_ref.shape[1], 256):
        span = slice(part, part + 256)
        mid_ref[:, span] = (
            dot_nt(glu_ref[EDGE:inner, :cols], glu_w_ref[0, span])
            + dot_nt(glu_ref[EDGE:inner, cols:], glu_w_ref[1, span])
        ).astype(LOW)


def front(place, out_rows, pre_rows, proj, input_rows, glu_weight, taps):
    frames, cols = pre_rows.shape
    wide = input_rows.shape[1]
    return call(
        front_kernel, "front",
        (place, out_rows, pre_rows, proj, input_rows, glu_weight, taps),
        [SMEM] + [VMEM] * 6,
        [
            shape((frames - 2 * EDGE, wide)), shape((frames, 2 * cols)), shape((frames, cols)),
            shape((4 * EDGE, cols)), shape((2 * EDGE, cols), FULL), shape((2 * EDGE, cols), FULL),
        ],
        scratch=[
            pltpu.VMEM((frames, cols), FULL), pltpu.VMEM((32, cols), FULL),
            pltpu.VMEM((frames, cols), FULL), pltpu.VMEM((frames, cols), FULL),
        ],
        flops=10 * frames * cols * wide, moved=6 * 2**20,
    )


def rim_kernel(
    place, before_ref, after_ref, rim_ref, gate_ref, value_ref, proj_ref, glu_w_ref, taps_ref, glu_in_ref,
    part_ref, glu_ref,
):
    del glu_in_ref
    frames = glu_ref.shape[0]
    cols = rim_ref.shape[1]
    first, length, total = place[0], place[1], place[2]
    out_rows = jnp.concatenate([before_ref[:EDGE], after_ref[:EDGE]], axis=0)
    pre_rows = jnp.concatenate([before_ref[EDGE:, :cols], after_ref[EDGE:, :cols]], axis=0)
    arrived = pre_grad(out_rows, pre_rows, proj_ref[...])[0].astype(FULL)
    above = jnp.where(first > 0, arrived[:EDGE], 0.0)
    below = jnp.where(first + frames < total, arrived[EDGE:], 0.0)
    own = rim_ref[...].astype(FULL)
    taps = taps_ref[...].astype(FULL)
    pieces = []
    for rows, start, place_of in (
        (jnp.concatenate([above, own[: 2 * EDGE]], axis=0), 0, slice(0, EDGE)),
        (jnp.concatenate([own[2 * EDGE :], below], axis=0), frames - EDGE, slice(EDGE, 2 * EDGE)),
    ):
        lows = []
        for part in range(0, cols, 128):
            span = slice(part, part + 128)
            frame = lax.broadcasted_iota(jnp.int32, (EDGE, 128), 0) + (first + start)
            grad_conv = jnp.where(frame < length, conv_strip(rows[:, span], taps[:, span]), 0.0)
            lows.append(glu_grads(grad_conv, gate_ref[place_of, span], value_ref[place_of, span]))
        low = jnp.concatenate([pair[0] for pair in lows] + [pair[1] for pair in lows], axis=1)
        glu_ref[start : start + EDGE] = low
        pieces.append(low)
    low = jnp.concatenate(pieces, axis=0)
    part_ref[...] = (dot_nt(low[:, :cols], glu_w_ref[0]) + dot_nt(low[:, cols:], glu_w_ref[1])).astype(LOW)


def rim(place, before, after, rim_rows, gate, value, proj, glu_weight, taps, glu_low):
    edge = pl.BlockSpec((2 * EDGE, before.shape[1]), lambda i: (WIN // (2 * EDGE), 0))
    whole = lambda array: pl.BlockSpec(array.shape, lambda i: (0,) * array.ndim)
    wide = glu_weight.shape[1]
    return call(
        rim_kernel, "rim",
        (place, before, after, rim_rows, gate, value, proj, glu_weight, taps, glu_low),
        [SMEM, edge, edge, whole(rim_rows), whole(gate), whole(value), VMEM, VMEM, whole(taps), VMEM],
        [shape((2 * EDGE, wide)), shape(glu_low.shape)],
        out_specs=[pl.BlockSpec((2 * EDGE, wide), lambda i: (0, 0)), VMEM],
        grid=(1,), input_output_aliases={9: 1},
        flops=2 * 32 * 1024 * 1536, moved=4 * 2**20,
    )


def terms_kernel(keeps, place, input_ref, glu_ref, out_ref, act_ref, *refs):
    sum_ref = refs[-1]
    core = place[3]
    wide = 2 * act_ref.shape[1]
    rows = sum_ref.shape[1]
    for half in range(2):
        block = 2 * half + (core if keeps else 1 - core)
        span = pl.ds(pl.multiple_of(block * rows, rows), rows)
        for source, low, start in ((input_ref, glu_ref, 0), (out_ref, act_ref, wide)):
            left = source[:, span]
            for part in range(0, low.shape[1], 256):
                term = dot_tn(left, low[:, part : part + 256])
                at = slice(start + part, start + part + 256)
                if keeps:
                    term = term + refs[0][half, :, at].astype(FULL)
                sum_ref[half, :, at] = term.astype(LOW)


def terms(place, input_rows, glu_low, out_rows, activated, arrived=None):
    wide = input_rows.shape[1]
    dims = (2, wide // 4, glu_low.shape[1] + activated.shape[1])
    operands = (place, input_rows, glu_low, out_rows, activated) + (() if arrived is None else (arrived,))
    return call(
        functools.partial(terms_kernel, arrived is not None), "terms",
        operands, [SMEM] + [VMEM] * (len(operands) - 1), [shape(dims)],
        flops=2 * input_rows.shape[0] * dims[0] * dims[1] * dims[2], moved=5 * 2**20,
    )[0]


def resid_kernel(
    place, out_ref, mid_ref, far_mid_ref, part_ref, far_part_ref, weight_ref, attended_ref,
    resid_ref, grad_ref, send_ref, keep_ref,
):
    frames = out_ref.shape[0]
    first, length, core = place[0], place[1], place[3]
    inner = frames - EDGE

    def total(rows, own, far):
        resid_ref[rows] = (out_ref[rows].astype(FULL) + (own.astype(FULL) + far.astype(FULL))).astype(LOW)

    total(slice(0, EDGE), part_ref[:EDGE], far_part_ref[:EDGE])
    total(slice(EDGE, inner), mid_ref[...], far_mid_ref[...])
    total(slice(inner, frames), part_ref[EDGE:], far_part_ref[EDGE:])
    rows = send_ref.shape[1]
    for out, flip in ((send_ref, 1), (keep_ref, 0)):
        for half in range(2):
            block = 2 * half + (1 - core if flip else core)
            span = pl.ds(pl.multiple_of(block * rows, rows), rows)
            out[half] = dot_tn(resid_ref[:, span], attended_ref[...]).astype(LOW)
    frame = lax.broadcasted_iota(jnp.int32, grad_ref.shape, 0) + first
    grad = dot_nt(resid_ref[...], weight_ref[...])
    grad_ref[...] = jnp.where(frame < length, grad, 0.0).astype(LOW)


def resid(place, out_rows, mid, far_mid, part, far_part, weight, attended):
    frames, wide = out_rows.shape
    cols = attended.shape[1]
    return call(
        resid_kernel, "resid",
        (place, out_rows, mid, far_mid, part, far_part, weight, attended),
        [SMEM] + [VMEM] * 7,
        [shape((frames, wide)), shape((frames, cols))] + [shape((2, wide // 4, cols))] * 2,
        flops=4 * frames * wide * cols, moved=6 * 2**20,
    )


def halves_kernel(place, own_ref, arrived_ref, send_ref, keep_ref):
    y_lo = place[4]
    for out, at in ((send_ref, 1 - y_lo), (keep_ref, y_lo)):
        out[...] = (own_ref[at].astype(FULL) + arrived_ref[at].astype(FULL)).astype(LOW)


def halves(place, own, arrived):
    return call(
        halves_kernel, "halves", (place, own, arrived), [SMEM, VMEM, VMEM], [shape(own.shape[1:])] * 2,
        moved=6 * own.size,
    )


BLOCK = 128
SPAN = BLOCK + 2 * WIN
SCALE = HEAD_DIM**-0.5
PAIR = 2 * HEAD_DIM


def side_by_side(rows):
    lane = lax.broadcasted_iota(jnp.int32, rows.shape, 1)
    zero = jnp.zeros_like(rows)
    return jnp.concatenate(
        [jnp.where(lane < HEAD_DIM, rows, zero), jnp.where(lane < HEAD_DIM, zero, rows)], axis=0
    )


def own_columns(columns):
    return jnp.concatenate([columns[:HEAD_DIM, :BLOCK], columns[HEAD_DIM:, BLOCK:]], axis=0)


def gather_rows(whole, before_ref, own_ref, after_ref, edge_span, span):
    frames = own_ref.shape[0]
    whole[:WIN] = before_ref[:WIN, edge_span]
    whole[WIN : WIN + frames] = own_ref[:, span]
    whole[WIN + frames :] = after_ref[:WIN, edge_span]


def spans(pair, cols):
    own = pl.ds(pl.multiple_of(pair * PAIR, PAIR), PAIR)
    far = pl.ds(pl.multiple_of(pair * PAIR + cols, PAIR), PAIR)
    return own, far


def attend_kernel(place, q_ref, k_ref, v_ref, before_ref, after_ref, prob_ref, out_ref, fill, keys, values):
    first, length = place[0], place[1]
    frames, cols = q_ref.shape
    for block in range(frames // BLOCK):
        key = lax.broadcasted_iota(jnp.int32, (SPAN, BLOCK), 0)
        offset = key - lax.broadcasted_iota(jnp.int32, (SPAN, BLOCK), 1)
        frame = key + (first - WIN + block * BLOCK)
        allowed = (offset >= 0) & (offset <= 2 * WIN) & (frame >= 0) & (frame < length)
        fill[block] = jnp.where(allowed, 0.0, NEG_FILL)

    def one_pair(pair, carry):
        own, far = spans(pair, cols)
        gather_rows(keys, before_ref, k_ref, after_ref, own, own)
        gather_rows(values, before_ref, v_ref, after_ref, far, own)
        for block in range(frames // BLOCK):
            rows = slice(block * BLOCK, (block + 1) * BLOCK)
            span = slice(block * BLOCK, block * BLOCK + SPAN)
            queries = side_by_side(q_ref[rows, own] * SCALE)
            scores = dot_nt(keys[span], queries) + jnp.concatenate([fill[block], fill[block]], axis=1)
            exponent = jnp.exp(scores - jnp.max(scores, axis=0, keepdims=True))
            prob = exponent * (1.0 / jnp.sum(exponent, axis=0, keepdims=True))
            prob_low = prob.astype(LOW)
            prob_ref[pair, block] = prob_low
            summed = own_columns(dot_tn(values[span], prob_low))
            frame = lax.broadcasted_iota(jnp.int32, (1, BLOCK), 1) + (first + block * BLOCK)
            out_ref[rows, own] = jnp.where(frame < length, summed, 0.0).T.astype(LOW)
        return carry

    lax.fori_loop(0, cols // PAIR, one_pair, 0)


def attend_grad_kernel(
    q_ref, k_ref, v_ref, before_ref, after_ref, prob_ref, out_ref, grad_ref,
    dq_ref, dk_ref, dv_ref, to_before_ref, to_after_ref, keys, values, key_sum, value_sum,
):
    frames, cols = q_ref.shape

    def one_pair(pair, carry):
        own, far = spans(pair, cols)
        gather_rows(keys, before_ref, k_ref, after_ref, own, own)
        gather_rows(values, before_ref, v_ref, after_ref, far, own)
        key_sum[...] = jnp.zeros_like(key_sum)
        value_sum[...] = jnp.zeros_like(value_sum)
        for block in range(frames // BLOCK):
            rows = slice(block * BLOCK, (block + 1) * BLOCK)
            span = slice(block * BLOCK, block * BLOCK + SPAN)
            queries = side_by_side(q_ref[rows, own] * SCALE)
            grad_rows = grad_ref[rows, own]
            grads = side_by_side(grad_rows)
            product = (grad_rows.astype(FULL) * out_ref[rows, own].astype(FULL)).T
            row_delta = jnp.concatenate(
                [
                    jnp.sum(product[:HEAD_DIM], axis=0, keepdims=True),
                    jnp.sum(product[HEAD_DIM:], axis=0, keepdims=True),
                ],
                axis=1,
            )
            prob_low = prob_ref[pair, block]
            grad_prob = dot_nt(values[span], grads)
            grad_score = (prob_low.astype(FULL) * (grad_prob - row_delta)).astype(LOW)
            value_sum[span] += jnp.dot(prob_low, grads, preferred_element_type=FULL)
            key_sum[span] += jnp.dot(grad_score, queries, preferred_element_type=FULL)
            dq_ref[rows, own] = (own_columns(dot_tn(keys[span], grad_score)).T * SCALE).astype(LOW)
        for total, inner, outer in ((key_sum, dk_ref, own), (value_sum, dv_ref, far)):
            to_before_ref[:, outer] = total[:WIN].astype(LOW)
            inner[:, own] = total[WIN : WIN + frames]
            to_after_ref[:, outer] = total[WIN + frames :].astype(LOW)
        return carry

    lax.fori_loop(0, cols // PAIR, one_pair, 0)


def attend(place, q_rows, k_rows, v_rows, before, after):
    frames, cols = q_rows.shape
    pairs, blocks = cols // PAIR, frames // BLOCK
    return call(
        attend_kernel, "attend", (place, q_rows, k_rows, v_rows, before, after), [SMEM] + [VMEM] * 5,
        [shape((pairs, blocks, SPAN, 2 * BLOCK)), shape((frames, cols))],
        scratch=[pltpu.VMEM((blocks, SPAN, BLOCK), FULL)] + [pltpu.VMEM((frames + 2 * WIN, PAIR), LOW)] * 2,
        flops=8 * frames * SPAN * cols, moved=6 * 2**20,
    )


def attend_grad(q_rows, k_rows, v_rows, before, after, prob, attended, grad_attn):
    frames, cols = q_rows.shape
    return call(
        attend_grad_kernel, "attend_grad",
        (q_rows, k_rows, v_rows, before, after, prob, attended, grad_attn), [VMEM] * 8,
        [shape((frames, cols))] + [shape((frames, cols), FULL)] * 2 + [shape((WIN, 2 * cols))] * 2,
        scratch=[pltpu.VMEM((frames + 2 * WIN, PAIR), LOW)] * 2 + [pltpu.VMEM((frames + 2 * WIN, PAIR), FULL)] * 2,
        flops=16 * frames * SPAN * cols, moved=9 * 2**20,
    )


def local(
    lengths,
    query_act,
    key_act,
    value_act,
    conv_input,
    conv_result,
    out_grad,
    out_weight,
    glu_weight,
    conv_taps,
    proj_weight,
):
    q_rows, k_rows, v_rows = (query_act[0], key_act[0], value_act[0])
    input_rows, pre_rows, out_rows = (conv_input[0], conv_result[0], out_grad[0])
    frames, cols = q_rows.shape
    peers = lax.axis_size("seq")
    index = lax.axis_index("dp")
    first = lax.axis_index("seq") * frames
    place = jnp.stack([first, lengths[0], peers * frames, index % 2, index // 2]).astype(jnp.int32)

    up, down = pack(k_rows, v_rows, out_rows, pre_rows)
    before, after = (round_ring(up, 1), round_ring(down, -1))
    mid, glu_low, activated, rim_rows, rim_gate, rim_value = front(
        place, out_rows, pre_rows, proj_weight, input_rows, glu_weight, conv_taps
    )
    far_mid = swapped(mid, "tensor", 1)
    part, glu_low = rim(
        place, before, after, rim_rows, rim_gate, rim_value, proj_weight, glu_weight, conv_taps, glu_low
    )
    far_part = swapped(part, "tensor", 1)
    given = swapped(terms(place, input_rows, glu_low, out_rows, activated), "dp", 1)
    prob, attended = attend(place, q_rows, k_rows, v_rows, before, after)
    on_chip = terms(place, input_rows, glu_low, out_rows, activated, given)
    resid_low, grad_attn, out_send, out_keep = resid(
        place, out_rows, mid, far_mid, part, far_part, out_weight, attended
    )
    out_given = swapped(out_send, "dp", 1)
    on_chip_out = halves(place, out_keep, out_given)
    on_chip_rest = halves(place, on_chip, jnp.zeros_like(on_chip))
    pair_out = on_chip_out[1].astype(FULL) + swapped(on_chip_out[0], "dp", 2).astype(FULL)
    pair_rest = on_chip_rest[1].astype(FULL) + swapped(on_chip_rest[0], "dp", 2).astype(FULL)
    grad_query, grad_key, grad_value, to_before, to_after = attend_grad(
        q_rows, k_rows, v_rows, before, after, prob, attended, grad_attn
    )
    from_after, from_before = (round_ring(to_before, -1), round_ring(to_after, 1))

    def with_arrived(own, span):
        below = jnp.pad(from_before[:, span].astype(FULL), ((0, frames - WIN), (0, 0)))
        above = jnp.pad(from_after[:, span].astype(FULL), ((frames - WIN, 0), (0, 0)))
        return (own + below + above).astype(LOW)

    joined = jnp.concatenate([pair_out, pair_rest], axis=1).astype(LOW)
    arrived = lax.all_to_all(joined.reshape(peers, -1, joined.shape[1]), "seq", 0, 0)
    summed = jnp.sum(arrived.astype(FULL), axis=0)
    glu_sum = summed[:, cols : 3 * cols].reshape(-1, 2, cols).transpose(1, 0, 2)
    return (
        resid_low[None],
        grad_query[None],
        with_arrived(grad_key, slice(0, cols))[None],
        with_arrived(grad_value, slice(cols, 2 * cols))[None],
        summed[:, :cols].T.astype(LOW),
        glu_sum.astype(LOW),
        summed[:, 3 * cols :].T.astype(LOW),
    )


def solution(mesh):
    in_specs = (
        P("dp"),
        P("dp", "seq", "tensor"),
        P("dp", "seq", "tensor"),
        P("dp", "seq", "tensor"),
        P("dp", "seq", None),
        P("dp", "seq", "tensor"),
        P("dp", "seq", None),
        P("tensor", None),
        P(None, None, "tensor"),
        P(None, "tensor"),
        P("tensor", None),
    )
    out_specs = (
        P("dp", "seq", None),
        P("dp", "seq", "tensor"),
        P("dp", "seq", "tensor"),
        P("dp", "seq", "tensor"),
        P("tensor", ("dp", "seq")),
        P(None, ("dp", "seq"), "tensor"),
        P("tensor", ("dp", "seq")),
    )
    return jax.shard_map(local, mesh=mesh, in_specs=in_specs, out_specs=out_specs, check_vma=False)
```

```python
import functools

import jax
import jax.numpy as jnp
from jax import lax
from jax.experimental import pallas as pl
from jax.experimental.pallas import tpu as pltpu
from jax.sharding import PartitionSpec as P

HEAD_DIM = 64
WIN = 256


NEG_FILL = -1e30
FULL, LOW = jnp.float32, jnp.bfloat16
TAPS = 31
EDGE = 16
STRIP = 32
VMEM = pl.BlockSpec(memory_space=pltpu.VMEM)
SMEM = pl.BlockSpec(memory_space=pltpu.SMEM)
HBM = pl.BlockSpec(memory_space=pltpu.HBM)


def shape(dims, kind=LOW):
    return jax.ShapeDtypeStruct(dims, kind)


def call(kernel, name, operands, in_specs, out_shape, out_specs=None, scratch=(), micros=1, limit=24, **more):
    return pl.pallas_call(
        kernel,
        in_specs=in_specs,
        out_specs=[VMEM] * len(out_shape) if out_specs is None else out_specs,
        out_shape=out_shape,
        scratch_shapes=list(scratch),
        compiler_params=pltpu.CompilerParams(vmem_limit_bytes=limit * 2**20),
        cost_estimate=pl.CostEstimate(flops=int(micros * 9e8), bytes_accessed=1, transcendentals=0),
        name=name,
        **more,
    )(*operands)


def whole(array):
    return pl.BlockSpec(array.shape, lambda i: (0,) * array.ndim)


def dot_nt(left, right):
    return lax.dot_general(left, right, (((1,), (1,)), ((), ())), preferred_element_type=FULL)


def dot_tn(left, right):
    return lax.dot_general(left, right, (((0,), (0,)), ((), ())), preferred_element_type=FULL)


def round_ring(value, steps):
    count = lax.axis_size("seq")
    return lax.ppermute(value, "seq", [(i, (i + steps) % count) for i in range(count)])


def swapped(value, axis, stride):
    count = lax.axis_size(axis)
    return lax.ppermute(value, axis, [(i, i ^ stride) for i in range(count)])


def pack_kernel(k_ref, v_ref, grad_ref, pre_ref, up_ref, down_ref, sems):
    frames, cols = k_ref.shape
    copies = []
    for out_ref, start, edge in ((up_ref, frames - WIN, frames - EDGE), (down_ref, 0, 0)):
        for source, rows, count, first, span in (
            (k_ref, 0, WIN, start, slice(0, cols)),
            (v_ref, 0, WIN, start, slice(cols, 2 * cols)),
            (grad_ref, WIN, EDGE, edge, slice(0, 2 * cols)),
            (pre_ref, WIN + EDGE, EDGE, edge, slice(0, cols)),
        ):
            copies.append(
                pltpu.make_async_copy(
                    source.at[pl.ds(first, count)], out_ref.at[pl.ds(rows, count), span], sems.at[len(copies)]
                )
            )
    for copy in copies:
        copy.start()
    for out_ref in (up_ref, down_ref):
        out_ref[WIN + EDGE :, cols:] = jnp.zeros((EDGE, cols), LOW)
    for copy in copies:
        copy.wait()


def pack(k_rows, v_rows, out_rows, pre_rows):
    dims = (WIN + 2 * EDGE, 2 * k_rows.shape[1])
    return call(
        pack_kernel, "pack", (k_rows, v_rows, out_rows, pre_rows), [HBM] * 4, [shape(dims)] * 2,
        scratch=[pltpu.SemaphoreType.DMA((8,))], limit=58,
    )


def pre_grad(out_rows, pre_rows, proj):
    pre = pre_rows.astype(FULL)
    logistic = jax.nn.sigmoid(pre)
    slope = logistic * (1.0 + pre * (1.0 - logistic))
    return (dot_nt(out_rows, proj) * slope).astype(LOW), (pre * logistic).astype(LOW)


def conv_strip(rows, taps):
    count = rows.shape[0] - 2 * EDGE
    total = jnp.zeros((count, rows.shape[1]), FULL)
    for shift in range(8):
        moved = rows[shift : shift + count + 24]
        for coarse in range(4):
            step = 8 * coarse + shift
            if step >= 1:
                total = total + taps[TAPS - step : TAPS - step + 1] * moved[8 * coarse : 8 * coarse + count]
    return total


def glu_grads(grad_conv, logistic, value):
    first = grad_conv * logistic
    return first.astype(LOW), (first * value * (1.0 - logistic)).astype(LOW)


def front_kernel(
    place, out_ref, pre_ref, proj_ref, input_ref, glu_w_ref, taps_ref,
    mid_ref, glu_ref, act_ref, rim_ref, rim_gate_ref, rim_value_ref,
    padded, taps, gates, values,
):
    frames, cols = pre_ref.shape
    first, length = place[0], place[1]
    inner = frames - EDGE
    taps[:TAPS] = taps_ref[...].astype(FULL)
    for part in range(0, cols, 256):
        span = slice(part, part + 256)
        grad_pre, activated = pre_grad(out_ref[...], pre_ref[:, span], proj_ref[span])
        act_ref[:, span] = activated
        padded[:, span] = grad_pre.astype(FULL)
        rim_ref[: 2 * EDGE, span] = grad_pre[: 2 * EDGE]
        rim_ref[2 * EDGE :, span] = grad_pre[frames - 2 * EDGE :]
        values[:, span] = jnp.dot(input_ref[...], glu_w_ref[0, :, span], preferred_element_type=FULL)
        gate_half = jnp.dot(input_ref[...], glu_w_ref[1, :, span], preferred_element_type=FULL)
        gates[:, span] = jax.nn.sigmoid(gate_half)
    for whole, rim in ((gates, rim_gate_ref), (values, rim_value_ref)):
        rim[:EDGE] = whole[:EDGE]
        rim[EDGE:] = whole[inner:]

    def strip(i, carry):
        at = pl.multiple_of(i * STRIP, STRIP)
        rows = pl.ds(pl.multiple_of(at + EDGE, EDGE), STRIP)
        frame = lax.broadcasted_iota(jnp.int32, (STRIP, 128), 0) + (first + EDGE + at)
        valid = frame < length
        for part in range(0, cols, 128):
            span = slice(part, part + 128)
            grad_conv = conv_strip(padded[pl.ds(at, STRIP + 2 * EDGE), span], taps[:, span])
            grad_conv = jnp.where(valid, grad_conv, 0.0)
            low = glu_grads(grad_conv, gates[rows, span], values[rows, span])
            glu_ref[rows, span] = low[0]
            glu_ref[rows, cols + part : cols + part + 128] = low[1]
        return carry

    lax.fori_loop(0, (frames - 2 * EDGE) // STRIP, strip, 0)
    for part in range(0, mid_ref.shape[1], 256):
        span = slice(part, part + 256)
        mid_ref[:, span] = (
            dot_nt(glu_ref[EDGE:inner, :cols], glu_w_ref[0, span])
            + dot_nt(glu_ref[EDGE:inner, cols:], glu_w_ref[1, span])
        ).astype(LOW)


def front(place, out_rows, pre_rows, proj, input_rows, glu_weight, taps):
    frames, cols = pre_rows.shape
    wide = input_rows.shape[1]
    return call(
        front_kernel, "front",
        (place, out_rows, pre_rows, proj, input_rows, glu_weight, taps),
        [SMEM] + [VMEM] * 6,
        [
            shape((frames - 2 * EDGE, wide)), shape((frames, 2 * cols)), shape((frames, cols)),
            shape((4 * EDGE, cols)), shape((2 * EDGE, cols), FULL), shape((2 * EDGE, cols), FULL),
        ],
        scratch=[
            pltpu.VMEM((frames, cols), FULL), pltpu.VMEM((32, cols), FULL),
            pltpu.VMEM((frames, cols), FULL), pltpu.VMEM((frames, cols), FULL),
        ],
        micros=7,
    )


def rim_kernel(
    place, before_ref, after_ref, rim_ref, gate_ref, value_ref, proj_ref, glu_w_ref, taps_ref, glu_in_ref,
    part_ref, glu_ref,
):
    frames = glu_ref.shape[0]
    cols = rim_ref.shape[1]
    first, length, total = place[0], place[1], place[2]
    glu_ref[EDGE : frames - EDGE] = glu_in_ref[EDGE : frames - EDGE]
    out_rows = jnp.concatenate([before_ref[:EDGE], after_ref[:EDGE]], axis=0)
    pre_rows = jnp.concatenate([before_ref[EDGE:, :cols], after_ref[EDGE:, :cols]], axis=0)
    arrived = pre_grad(out_rows, pre_rows, proj_ref[...])[0].astype(FULL)
    above = jnp.where(first > 0, arrived[:EDGE], 0.0)
    below = jnp.where(first + frames < total, arrived[EDGE:], 0.0)
    own = rim_ref[...].astype(FULL)
    taps = taps_ref[...].astype(FULL)
    pieces = []
    for rows, start, place_of in (
        (jnp.concatenate([above, own[: 2 * EDGE]], axis=0), 0, slice(0, EDGE)),
        (jnp.concatenate([own[2 * EDGE :], below], axis=0), frames - EDGE, slice(EDGE, 2 * EDGE)),
    ):
        lows = []
        for part in range(0, cols, 128):
            span = slice(part, part + 128)
            frame = lax.broadcasted_iota(jnp.int32, (EDGE, 128), 0) + (first + start)
            grad_conv = jnp.where(frame < length, conv_strip(rows[:, span], taps[:, span]), 0.0)
            lows.append(glu_grads(grad_conv, gate_ref[place_of, span], value_ref[place_of, span]))
        low = jnp.concatenate([pair[0] for pair in lows] + [pair[1] for pair in lows], axis=1)
        glu_ref[start : start + EDGE] = low
        pieces.append(low)
    low = jnp.concatenate(pieces, axis=0)
    part_ref[...] = (dot_nt(low[:, :cols], glu_w_ref[0]) + dot_nt(low[:, cols:], glu_w_ref[1])).astype(LOW)


def rim(place, before, after, rim_rows, gate, value, proj, glu_weight, taps, glu_low):
    edge = pl.BlockSpec((2 * EDGE, before.shape[1]), lambda i: (WIN // (2 * EDGE), 0))
    wide = glu_weight.shape[1]
    return call(
        rim_kernel, "rim",
        (place, before, after, rim_rows, gate, value, proj, glu_weight, taps, glu_low),
        [SMEM, edge, edge, whole(rim_rows), whole(gate), whole(value), VMEM, VMEM, whole(taps), VMEM],
        [shape((2 * EDGE, wide)), shape(glu_low.shape)],
        out_specs=[pl.BlockSpec((2 * EDGE, wide), lambda i: (0, 0)), VMEM],
        grid=(1,), micros=0.1,
    )


def terms_kernel(keeps, place, input_ref, glu_ref, out_ref, act_ref, *refs):
    core = place[3]
    cols = act_ref.shape[1]
    rows = input_ref.shape[1] // 4
    peers = 4
    sources = ((input_ref, glu_ref, 0), (input_ref, glu_ref, cols), (out_ref, act_ref, 0))
    for half in range(2):
        block = 2 * half + (core if keeps else 1 - core)
        span = pl.ds(pl.multiple_of(block * rows, rows), rows)
        for which, (source, low, start) in enumerate(sources):
            left = source[:, span]
            for part in range(0, cols, 256):
                term = dot_tn(left, low[:, start + part : start + part + 256])
                at = slice(part, part + 256)
                if not keeps:
                    refs[which][half, :, at] = term.astype(LOW)
                    continue
                term = term + refs[which][half, :, at].astype(FULL)
                at = slice(cols * which + part, cols * which + part + 256)
                for peer, moved in enumerate(by_peer(term, peers)):
                    refs[3][half, peer, :, at] = moved.astype(LOW)


def terms(place, input_rows, glu_low, out_rows, activated, arrived=()):
    wide, cols = input_rows.shape[1], activated.shape[1]
    out_shape = [shape((2, 4, wide // 16, 3 * cols))] if arrived else [shape((2, wide // 4, cols))] * 3
    operands = (place, input_rows, glu_low, out_rows, activated) + tuple(arrived)
    return call(
        functools.partial(terms_kernel, bool(arrived)), "terms",
        operands, [SMEM] + [VMEM] * (len(operands) - 1), out_shape, micros=0.1,
    )


def resid_kernel(
    place, out_ref, mid_ref, far_mid_ref, part_ref, far_part_ref, weight_ref, attended_ref,
    resid_ref, grad_ref, send_ref, keep_ref,
):
    frames = out_ref.shape[0]
    first, length, core = place[0], place[1], place[3]
    inner = frames - EDGE

    def total(rows, own, far):
        resid_ref[rows] = (out_ref[rows].astype(FULL) + (own.astype(FULL) + far.astype(FULL))).astype(LOW)

    total(slice(0, EDGE), part_ref[:EDGE], far_part_ref[:EDGE])
    total(slice(EDGE, inner), mid_ref[...], far_mid_ref[...])
    total(slice(inner, frames), part_ref[EDGE:], far_part_ref[EDGE:])
    rows = send_ref.shape[1]
    for out, flip in ((send_ref, 1), (keep_ref, 0)):
        for half in range(2):
            block = 2 * half + (1 - core if flip else core)
            span = pl.ds(pl.multiple_of(block * rows, rows), rows)
            out[half] = dot_tn(resid_ref[:, span], attended_ref[...]).astype(LOW)
    frame = lax.broadcasted_iota(jnp.int32, grad_ref.shape, 0) + first
    grad = dot_nt(resid_ref[...], weight_ref[...])
    grad_ref[...] = jnp.where(frame < length, grad, 0.0).astype(LOW)


def resid(place, out_rows, mid, far_mid, part, far_part, weight, attended):
    frames, wide = out_rows.shape
    cols = attended.shape[1]
    return call(
        resid_kernel, "resid",
        (place, out_rows, mid, far_mid, part, far_part, weight, attended),
        [SMEM] + [whole(a) for a in (out_rows, mid, far_mid, part, far_part, weight, attended)],
        [shape((frames, wide)), shape((frames, cols))] + [shape((2, wide // 4, cols))] * 2,
        out_specs=[whole(a) for a in (out_rows, attended)]
        + [pl.BlockSpec((2, wide // 4, cols), lambda i: (0, 0, 0))] * 2,
        grid=(1,), micros=60, limit=58,
    )


def by_peer(rows, peers):
    groups = rows.reshape(rows.shape[0] // (8 * peers), peers, 8, rows.shape[1])
    return [groups[:, peer].reshape(-1, rows.shape[1]) for peer in range(peers)]


def add_kernel(own_ref, arrived_ref, sum_ref):
    for half in range(2):
        total = own_ref[half].astype(FULL) + arrived_ref[half].astype(FULL)
        for peer, rows in enumerate(by_peer(total, sum_ref.shape[1])):
            sum_ref[half, peer] = rows.astype(LOW)


def add(own, arrived, peers):
    halves, rows, cols = own.shape
    return call(add_kernel, "add", (own, arrived), [VMEM, VMEM], [shape((halves, peers, rows // peers, cols))])[0]


def plane_kernel(*refs):
    *sources, sum_ref = refs
    at = 0
    for parts_ref in sources:
        for start in range(0, parts_ref.shape[2], 512):
            span = slice(start, start + 512)
            total = parts_ref[0, :, span].astype(FULL)
            for i in range(1, parts_ref.shape[0]):
                total = total + parts_ref[i, :, span].astype(FULL)
            sum_ref[:, at : at + 512] = total.astype(LOW)
            at += 512


def plane_sum(*parts):
    dims = (parts[0].shape[1], sum(part.shape[2] for part in parts))
    return call(plane_kernel, "plane_sum", parts, [VMEM] * len(parts), [shape(dims)])[0]


def line_kernel(parts_ref, out_ref, glu_ref, proj_ref):
    total = parts_ref[0].astype(FULL)
    for i in range(1, parts_ref.shape[0]):
        total = total + parts_ref[i].astype(FULL)
    cols = out_ref.shape[1]
    glu_ref[0] = total[:, :cols].astype(LOW)
    glu_ref[1] = total[:, cols : 2 * cols].astype(LOW)
    proj_ref[...] = total[:, 2 * cols : 3 * cols].astype(LOW)
    out_ref[...] = total[:, 3 * cols :].astype(LOW)


def line_sum(parts):
    rows, cols = parts.shape[1], parts.shape[2] // 4
    return call(
        line_kernel, "line_sum", (parts,), [VMEM], [shape((rows, cols)), shape((2, rows, cols)), shape((rows, cols))]
    )


def exchanged(parts, groups):
    return lax.all_to_all(parts, ("dp", "seq"), 0, 0, axis_index_groups=groups)


BLOCK = 128
SPAN = BLOCK + 2 * WIN
SCALE = HEAD_DIM**-0.5
PAIR = 2 * HEAD_DIM


def side_by_side(rows):
    lane = lax.broadcasted_iota(jnp.int32, rows.shape, 1)
    zero = jnp.zeros_like(rows)
    return jnp.concatenate(
        [jnp.where(lane < HEAD_DIM, rows, zero), jnp.where(lane < HEAD_DIM, zero, rows)], axis=0
    )


def own_columns(columns):
    return jnp.concatenate([columns[:HEAD_DIM, :BLOCK], columns[HEAD_DIM:, BLOCK:]], axis=0)


def gather_rows(whole, before_ref, own_ref, after_ref):
    frames = own_ref.shape[0]
    whole[:WIN] = before_ref[...]
    whole[WIN : WIN + frames] = own_ref[...]
    whole[WIN + frames :] = after_ref[...]


def pair_specs(frames, pairs):
    own = pl.BlockSpec((frames, PAIR), lambda i: (0, i))
    far_key = pl.BlockSpec((WIN, PAIR), lambda i: (0, i))
    far_value = pl.BlockSpec((WIN, PAIR), lambda i: (0, i + pairs))
    return own, far_key, far_value


def attend_kernel(
    place, q_ref, k_ref, v_ref, kb_ref, vb_ref, ka_ref, va_ref, prob_ref, out_ref, fill, keys, values
):
    first, length = place[0], place[1]
    frames = q_ref.shape[0]

    @pl.when(pl.program_id(0) == 0)
    def _():
        for block in range(frames // BLOCK):
            key = lax.broadcasted_iota(jnp.int32, (SPAN, BLOCK), 0)
            offset = key - lax.broadcasted_iota(jnp.int32, (SPAN, BLOCK), 1)
            frame = key + (first - WIN + block * BLOCK)
            allowed = (offset >= 0) & (offset <= 2 * WIN) & (frame >= 0) & (frame < length)
            fill[block] = jnp.where(allowed, 0.0, NEG_FILL)

    gather_rows(keys, kb_ref, k_ref, ka_ref)
    gather_rows(values, vb_ref, v_ref, va_ref)
    for block in range(frames // BLOCK):
        rows = slice(block * BLOCK, (block + 1) * BLOCK)
        span = slice(block * BLOCK, block * BLOCK + SPAN)
        queries = side_by_side(q_ref[rows] * SCALE)
        scores = dot_nt(keys[span], queries) + jnp.concatenate([fill[block], fill[block]], axis=1)
        exponent = jnp.exp(scores - jnp.max(scores, axis=0, keepdims=True))
        prob = exponent * (1.0 / jnp.sum(exponent, axis=0, keepdims=True))
        prob_low = prob.astype(LOW)
        prob_ref[0, block] = prob_low
        summed = own_columns(dot_tn(values[span], prob_low))
        frame = lax.broadcasted_iota(jnp.int32, (1, BLOCK), 1) + (first + block * BLOCK)
        out_ref[rows] = jnp.where(frame < length, summed, 0.0).T.astype(LOW)


def attend_grad_kernel(
    q_ref, k_ref, v_ref, kb_ref, vb_ref, ka_ref, va_ref, prob_ref, out_ref, grad_ref,
    dq_ref, dk_ref, dv_ref, to_before_ref, to_after_ref, keys, values, key_sum, value_sum,
):
    frames = q_ref.shape[0]
    gather_rows(keys, kb_ref, k_ref, ka_ref)
    gather_rows(values, vb_ref, v_ref, va_ref)
    key_sum[...] = jnp.zeros_like(key_sum)
    value_sum[...] = jnp.zeros_like(value_sum)
    for block in range(frames // BLOCK):
        rows = slice(block * BLOCK, (block + 1) * BLOCK)
        span = slice(block * BLOCK, block * BLOCK + SPAN)
        queries = side_by_side(q_ref[rows] * SCALE)
        grad_rows = grad_ref[rows]
        grads = side_by_side(grad_rows)
        product = (grad_rows.astype(FULL) * out_ref[rows].astype(FULL)).T
        row_delta = jnp.concatenate(
            [
                jnp.sum(product[:HEAD_DIM], axis=0, keepdims=True),
                jnp.sum(product[HEAD_DIM:], axis=0, keepdims=True),
            ],
            axis=1,
        )
        prob_low = prob_ref[0, block]
        grad_prob = dot_nt(values[span], grads)
        grad_score = (prob_low.astype(FULL) * (grad_prob - row_delta)).astype(LOW)
        value_sum[span] += jnp.dot(prob_low, grads, preferred_element_type=FULL)
        key_sum[span] += jnp.dot(grad_score, queries, preferred_element_type=FULL)
        dq_ref[rows] = (own_columns(dot_tn(keys[span], grad_score)).T * SCALE).astype(LOW)
    for total, inner, lane in ((key_sum, dk_ref, 0), (value_sum, dv_ref, PAIR)):
        to_before_ref[:, lane : lane + PAIR] = total[:WIN].astype(LOW)
        inner[...] = total[WIN : WIN + frames]
        to_after_ref[:, lane : lane + PAIR] = total[WIN + frames :].astype(LOW)


def attend(place, q_rows, k_rows, v_rows, before, after):
    frames, cols = q_rows.shape
    pairs, blocks = cols // PAIR, frames // BLOCK
    own, far_key, far_value = pair_specs(frames, pairs)
    return call(
        attend_kernel, "attend", (place, q_rows, k_rows, v_rows, before, before, after, after),
        [SMEM, own, own, own, far_key, far_value, far_key, far_value],
        [shape((pairs, blocks, SPAN, 2 * BLOCK)), shape((frames, cols))],
        out_specs=[pl.BlockSpec((1, blocks, SPAN, 2 * BLOCK), lambda i: (i, 0, 0, 0)), own],
        scratch=[pltpu.VMEM((blocks, SPAN, BLOCK), FULL)] + [pltpu.VMEM((frames + 2 * WIN, PAIR), LOW)] * 2,
        grid=(pairs,), micros=0.5, limit=58,
    )


def attend_grad(q_rows, k_rows, v_rows, before, after, prob, attended, grad_attn):
    frames, cols = q_rows.shape
    pairs, blocks = cols // PAIR, frames // BLOCK
    own, far_key, far_value = pair_specs(frames, pairs)
    far = pl.BlockSpec((WIN, 2 * PAIR), lambda i: (0, i))
    return call(
        attend_grad_kernel, "attend_grad",
        (q_rows, k_rows, v_rows, before, before, after, after, prob, attended, grad_attn),
        [own, own, own, far_key, far_value, far_key, far_value]
        + [pl.BlockSpec((1, blocks, SPAN, 2 * BLOCK), lambda i: (i, 0, 0, 0)), own, own],
        [shape((frames, cols))] + [shape((frames, cols), FULL)] * 2 + [shape((WIN, 2 * cols))] * 2,
        out_specs=[own, own, own, far, far],
        scratch=[pltpu.VMEM((frames + 2 * WIN, PAIR), LOW)] * 2 + [pltpu.VMEM((frames + 2 * WIN, PAIR), FULL)] * 2,
        grid=(pairs,), micros=50, limit=58,
    )


def finish_kernel(dk_ref, dv_ref, from_before_ref, from_after_ref, key_ref, value_ref):
    frames, cols = dk_ref.shape
    shared = frames - WIN
    for own, out, lane in ((dk_ref, key_ref, 0), (dv_ref, value_ref, PAIR)):
        for start in range(0, cols, PAIR):
            span = slice(start, start + PAIR)
            far_span = slice(2 * start + lane, 2 * start + lane + PAIR)
            above = own[:WIN, span] + from_before_ref[:, far_span].astype(FULL)
            far = from_after_ref[:, far_span].astype(FULL)
            out[:shared, span] = above[:shared].astype(LOW)
            out[shared:WIN, span] = (above[shared:] + far[: WIN - shared]).astype(LOW)
            out[WIN:, span] = (own[WIN:, span] + far[WIN - shared :]).astype(LOW)


def finish(grad_key, grad_value, from_before, from_after):
    own = pl.BlockSpec(grad_key.shape, lambda i: (0, 0))
    far = pl.BlockSpec(from_before.shape, lambda i: (0, 0))
    return call(
        finish_kernel, "finish", (grad_key, grad_value, from_before, from_after), [own, own, far, far],
        [shape(grad_key.shape)] * 2, out_specs=[own, own], grid=(1,), micros=2, limit=58,
    )


def local(
    lengths,
    query_act,
    key_act,
    value_act,
    conv_input,
    conv_result,
    out_grad,
    out_weight,
    glu_weight,
    conv_taps,
    proj_weight,
):
    q_rows, k_rows, v_rows = (query_act[0], key_act[0], value_act[0])
    input_rows, pre_rows, out_rows = (conv_input[0], conv_result[0], out_grad[0])
    frames, cols = q_rows.shape
    peers = lax.axis_size("seq")
    index = lax.axis_index("dp")
    first = lax.axis_index("seq") * frames
    place = jnp.stack([first, lengths[0], peers * frames, index % 2, index // 2]).astype(jnp.int32)

    up, down = pack(k_rows, v_rows, out_rows, pre_rows)
    before, after = (round_ring(up, 1), round_ring(down, -1))
    mid, glu_low, activated, rim_rows, rim_gate, rim_value = front(
        place, out_rows, pre_rows, proj_weight, input_rows, glu_weight, conv_taps
    )
    far_mid = swapped(mid, "tensor", 1)
    part, glu_low = rim(
        place, before, after, rim_rows, rim_gate, rim_value, proj_weight, glu_weight, conv_taps, glu_low
    )
    far_part = swapped(part, "tensor", 1)
    given = [swapped(term, "dp", 1) for term in terms(place, input_rows, glu_low, out_rows, activated)]
    on_chip = terms(place, input_rows, glu_low, out_rows, activated, given)[0]
    q_late, on_chip = lax.optimization_barrier((q_rows, on_chip))
    prob, attended = attend(place, q_late, k_rows, v_rows, before, after)
    resid_low, grad_attn, out_send, out_keep = resid(
        place, out_rows, mid, far_mid, part, far_part, out_weight, attended
    )
    xs, zs, pairs, cores = (4, peers // 4, range(2), range(2))
    by_plane = [
        [(2 * y + core) * peers + z * xs + x for y in pairs for x in range(xs)]
        for core in cores for z in range(zs)
    ]
    by_line = [[d * peers + z * xs + x for z in range(zs)] for d in range(4) for x in range(xs)]
    rest = exchanged(on_chip.reshape((2 * xs,) + on_chip.shape[2:]), by_plane)
    on_chip_out = add(out_keep, swapped(out_send, "dp", 1), xs)
    on_chip_out, rest = lax.optimization_barrier((on_chip_out, rest))
    outs = exchanged(on_chip_out.reshape((2 * xs,) + on_chip_out.shape[2:]), by_plane)
    plane = plane_sum(rest, outs)
    out_sum, glu_sum, proj_sum = line_sum(exchanged(plane.reshape(zs, -1, plane.shape[1]), by_line))
    grad_query, grad_key, grad_value, to_before, to_after = attend_grad(
        q_rows, k_rows, v_rows, before, after, prob, attended, grad_attn
    )
    from_after, from_before = (round_ring(to_before, -1), round_ring(to_after, 1))

    key_grad, value_grad = finish(grad_key, grad_value, from_before, from_after)
    return (
        resid_low[None],
        grad_query[None],
        key_grad[None],
        value_grad[None],
        out_sum.T,
        glu_sum,
        proj_sum.T,
    )


def solution(mesh):
    in_specs = (
        P("dp"),
        P("dp", "seq", "tensor"),
        P("dp", "seq", "tensor"),
        P("dp", "seq", "tensor"),
        P("dp", "seq", None),
        P("dp", "seq", "tensor"),
        P("dp", "seq", None),
        P("tensor", None),
        P(None, None, "tensor"),
        P(None, "tensor"),
        P("tensor", None),
    )
    out_specs = (
        P("dp", "seq", None),
        P("dp", "seq", "tensor"),
        P("dp", "seq", "tensor"),
        P("dp", "seq", "tensor"),
        P("tensor", ("dp", "seq")),
        P(None, ("dp", "seq"), "tensor"),
        P("tensor", ("dp", "seq")),
    )
    return jax.shard_map(local, mesh=mesh, in_specs=in_specs, out_specs=out_specs, check_vma=False)
```

```python
import functools

import jax
import jax.numpy as jnp
from jax import lax
from jax.experimental import pallas as pl
from jax.experimental.pallas import tpu as pltpu
from jax.sharding import PartitionSpec as P

HEAD_DIM = 64
WIN = 256


NEG_FILL = -1e30
FULL, LOW = jnp.float32, jnp.bfloat16
TAPS = 31
EDGE = 16
STRIP = 32
VMEM = pl.BlockSpec(memory_space=pltpu.VMEM)
SMEM = pl.BlockSpec(memory_space=pltpu.SMEM)
HBM = pl.BlockSpec(memory_space=pltpu.HBM)


def shape(dims, kind=LOW):
    return jax.ShapeDtypeStruct(dims, kind)


def call(kernel, name, operands, in_specs, out_shape, out_specs=None, scratch=(), micros=1, limit=24, **more):
    return pl.pallas_call(
        kernel,
        in_specs=in_specs,
        out_specs=[VMEM] * len(out_shape) if out_specs is None else out_specs,
        out_shape=out_shape,
        scratch_shapes=list(scratch),
        compiler_params=pltpu.CompilerParams(vmem_limit_bytes=limit * 2**20),
        cost_estimate=pl.CostEstimate(flops=int(micros * 9e8), bytes_accessed=1, transcendentals=0),
        name=name,
        **more,
    )(*operands)


def whole(array):
    return pl.BlockSpec(array.shape, lambda i: (0,) * array.ndim)


def dot_nt(left, right):
    return lax.dot_general(left, right, (((1,), (1,)), ((), ())), preferred_element_type=FULL)


def dot_tn(left, right):
    return lax.dot_general(left, right, (((0,), (0,)), ((), ())), preferred_element_type=FULL)


def round_ring(value, steps):
    count = lax.axis_size("seq")
    return lax.ppermute(value, "seq", [(i, (i + steps) % count) for i in range(count)])


def swapped(value, axis, stride):
    count = lax.axis_size(axis)
    return lax.ppermute(value, axis, [(i, i ^ stride) for i in range(count)])


def pack_kernel(k_ref, v_ref, grad_ref, pre_ref, up_ref, down_ref, sems):
    frames, cols = k_ref.shape
    copies = []
    for out_ref, start, edge in ((up_ref, frames - WIN, frames - EDGE), (down_ref, 0, 0)):
        for source, rows, count, first, span in (
            (k_ref, 0, WIN, start, slice(0, cols)),
            (v_ref, 0, WIN, start, slice(cols, 2 * cols)),
            (grad_ref, WIN, EDGE, edge, slice(0, 2 * cols)),
            (pre_ref, WIN + EDGE, EDGE, edge, slice(0, cols)),
        ):
            copies.append(
                pltpu.make_async_copy(
                    source.at[pl.ds(first, count)], out_ref.at[pl.ds(rows, count), span], sems.at[len(copies)]
                )
            )
    for copy in copies:
        copy.start()
    for out_ref in (up_ref, down_ref):
        out_ref[WIN + EDGE :, cols:] = jnp.zeros((EDGE, cols), LOW)
    for copy in copies:
        copy.wait()


def pack(k_rows, v_rows, out_rows, pre_rows):
    dims = (WIN + 2 * EDGE, 2 * k_rows.shape[1])
    return call(
        pack_kernel, "pack", (k_rows, v_rows, out_rows, pre_rows), [HBM] * 4, [shape(dims)] * 2,
        scratch=[pltpu.SemaphoreType.DMA((8,))], limit=58,
    )


def pre_grad(out_rows, pre_rows, proj):
    pre = pre_rows.astype(FULL)
    logistic = jax.nn.sigmoid(pre)
    slope = logistic * (1.0 + pre * (1.0 - logistic))
    return (dot_nt(out_rows, proj) * slope).astype(LOW), (pre * logistic).astype(LOW)


def conv_strip(rows, taps):
    count = rows.shape[0] - 2 * EDGE
    total = jnp.zeros((count, rows.shape[1]), FULL)
    for shift in range(8):
        moved = rows[shift : shift + count + 24]
        for coarse in range(4):
            step = 8 * coarse + shift
            if step >= 1:
                total = total + taps[TAPS - step : TAPS - step + 1] * moved[8 * coarse : 8 * coarse + count]
    return total


def glu_grads(grad_conv, logistic, value):
    first = grad_conv * logistic
    return first.astype(LOW), (first * value * (1.0 - logistic)).astype(LOW)


def front_kernel(
    place, out_ref, pre_ref, proj_ref, input_ref, glu_w_ref, taps_ref,
    mid_ref, glu_ref, act_ref, rim_ref, rim_gate_ref, rim_value_ref,
    padded, taps, gates, values,
):
    frames, cols = pre_ref.shape
    first, length = place[0], place[1]
    inner = frames - EDGE
    taps[:TAPS] = taps_ref[...].astype(FULL)
    for part in range(0, cols, 256):
        span = slice(part, part + 256)
        grad_pre, activated = pre_grad(out_ref[...], pre_ref[:, span], proj_ref[span])
        act_ref[:, span] = activated
        padded[:, span] = grad_pre.astype(FULL)
        rim_ref[: 2 * EDGE, span] = grad_pre[: 2 * EDGE]
        rim_ref[2 * EDGE :, span] = grad_pre[frames - 2 * EDGE :]
        values[:, span] = jnp.dot(input_ref[...], glu_w_ref[0, :, span], preferred_element_type=FULL)
        gate_half = jnp.dot(input_ref[...], glu_w_ref[1, :, span], preferred_element_type=FULL)
        gates[:, span] = jax.nn.sigmoid(gate_half)
    for whole, rim in ((gates, rim_gate_ref), (values, rim_value_ref)):
        rim[:EDGE] = whole[:EDGE]
        rim[EDGE:] = whole[inner:]

    def strip(i, carry):
        at = pl.multiple_of(i * STRIP, STRIP)
        rows = pl.ds(pl.multiple_of(at + EDGE, EDGE), STRIP)
        frame = lax.broadcasted_iota(jnp.int32, (STRIP, 128), 0) + (first + EDGE + at)
        valid = frame < length
        for part in range(0, cols, 128):
            span = slice(part, part + 128)
            grad_conv = conv_strip(padded[pl.ds(at, STRIP + 2 * EDGE), span], taps[:, span])
            grad_conv = jnp.where(valid, grad_conv, 0.0)
            low = glu_grads(grad_conv, gates[rows, span], values[rows, span])
            glu_ref[rows, span] = low[0]
            glu_ref[rows, cols + part : cols + part + 128] = low[1]
        return carry

    lax.fori_loop(0, (frames - 2 * EDGE) // STRIP, strip, 0)
    for part in range(0, mid_ref.shape[1], 256):
        span = slice(part, part + 256)
        mid_ref[:, span] = (
            dot_nt(glu_ref[EDGE:inner, :cols], glu_w_ref[0, span])
            + dot_nt(glu_ref[EDGE:inner, cols:], glu_w_ref[1, span])
        ).astype(LOW)


def front(place, out_rows, pre_rows, proj, input_rows, glu_weight, taps):
    frames, cols = pre_rows.shape
    wide = input_rows.shape[1]
    return call(
        front_kernel, "front",
        (place, out_rows, pre_rows, proj, input_rows, glu_weight, taps),
        [SMEM] + [VMEM] * 6,
        [
            shape((frames - 2 * EDGE, wide)), shape((frames, 2 * cols)), shape((frames, cols)),
            shape((4 * EDGE, cols)), shape((2 * EDGE, cols), FULL), shape((2 * EDGE, cols), FULL),
        ],
        scratch=[
            pltpu.VMEM((frames, cols), FULL), pltpu.VMEM((32, cols), FULL),
            pltpu.VMEM((frames, cols), FULL), pltpu.VMEM((frames, cols), FULL),
        ],
        micros=7,
    )


def rim_kernel(
    place, before_ref, after_ref, rim_ref, gate_ref, value_ref, proj_ref, glu_w_ref, taps_ref, glu_in_ref,
    part_ref, glu_ref,
):
    frames = glu_ref.shape[0]
    cols = rim_ref.shape[1]
    first, length, total = place[0], place[1], place[2]
    glu_ref[EDGE : frames - EDGE] = glu_in_ref[EDGE : frames - EDGE]
    out_rows = jnp.concatenate([before_ref[:EDGE], after_ref[:EDGE]], axis=0)
    pre_rows = jnp.concatenate([before_ref[EDGE:, :cols], after_ref[EDGE:, :cols]], axis=0)
    arrived = pre_grad(out_rows, pre_rows, proj_ref[...])[0].astype(FULL)
    above = jnp.where(first > 0, arrived[:EDGE], 0.0)
    below = jnp.where(first + frames < total, arrived[EDGE:], 0.0)
    own = rim_ref[...].astype(FULL)
    taps = taps_ref[...].astype(FULL)
    pieces = []
    for rows, start, place_of in (
        (jnp.concatenate([above, own[: 2 * EDGE]], axis=0), 0, slice(0, EDGE)),
        (jnp.concatenate([own[2 * EDGE :], below], axis=0), frames - EDGE, slice(EDGE, 2 * EDGE)),
    ):
        lows = []
        for part in range(0, cols, 128):
            span = slice(part, part + 128)
            frame = lax.broadcasted_iota(jnp.int32, (EDGE, 128), 0) + (first + start)
            grad_conv = jnp.where(frame < length, conv_strip(rows[:, span], taps[:, span]), 0.0)
            lows.append(glu_grads(grad_conv, gate_ref[place_of, span], value_ref[place_of, span]))
        low = jnp.concatenate([pair[0] for pair in lows] + [pair[1] for pair in lows], axis=1)
        glu_ref[start : start + EDGE] = low
        pieces.append(low)
    low = jnp.concatenate(pieces, axis=0)
    part_ref[...] = (dot_nt(low[:, :cols], glu_w_ref[0]) + dot_nt(low[:, cols:], glu_w_ref[1])).astype(LOW)


def rim(place, before, after, rim_rows, gate, value, proj, glu_weight, taps, glu_low):
    edge = pl.BlockSpec((2 * EDGE, before.shape[1]), lambda i: (WIN // (2 * EDGE), 0))
    wide = glu_weight.shape[1]
    return call(
        rim_kernel, "rim",
        (place, before, after, rim_rows, gate, value, proj, glu_weight, taps, glu_low),
        [SMEM, edge, edge, whole(rim_rows), whole(gate), whole(value), VMEM, VMEM, whole(taps), VMEM],
        [shape((2 * EDGE, wide)), shape(glu_low.shape)],
        out_specs=[pl.BlockSpec((2 * EDGE, wide), lambda i: (0, 0)), VMEM],
        grid=(1,), micros=0.1,
    )


def terms_kernel(keeps, place, input_ref, glu_ref, out_ref, act_ref, *refs):
    core = place[3]
    cols = act_ref.shape[1]
    rows = input_ref.shape[1] // 4
    peers = 8
    sources = ((input_ref, glu_ref, 0), (input_ref, glu_ref, cols), (out_ref, act_ref, 0))
    for half in range(2):
        block = 2 * half + (core if keeps else 1 - core)
        span = pl.ds(pl.multiple_of(block * rows, rows), rows)
        for which, (source, low, start) in enumerate(sources):
            left = source[:, span]
            for part in range(0, cols, 256):
                term = dot_tn(left, low[:, start + part : start + part + 256])
                at = slice(part, part + 256)
                if not keeps:
                    refs[which][half, :, at] = term.astype(LOW)
                    continue
                term = term + refs[which][half, :, at].astype(FULL)
                at = slice(cols * which + part, cols * which + part + 256)
                share = rows // peers
                for peer, moved in enumerate(by_peer(term, peers)):
                    refs[3][peer, half * share : (half + 1) * share, at] = moved.astype(LOW)


def terms(place, input_rows, glu_low, out_rows, activated, arrived=()):
    wide, cols = input_rows.shape[1], activated.shape[1]
    out_shape = [shape((8, wide // 16, 3 * cols))] if arrived else [shape((2, wide // 4, cols))] * 3
    operands = (place, input_rows, glu_low, out_rows, activated) + tuple(arrived)
    return call(
        functools.partial(terms_kernel, bool(arrived)), "terms",
        operands, [SMEM] + [VMEM] * (len(operands) - 1), out_shape, micros=0.1,
    )


def resid_kernel(
    place, out_ref, mid_ref, far_mid_ref, part_ref, far_part_ref, weight_ref, attended_ref,
    resid_ref, grad_ref, send_ref, keep_ref,
):
    frames = out_ref.shape[0]
    first, length, core = place[0], place[1], place[3]
    inner = frames - EDGE

    def total(rows, own, far):
        resid_ref[rows] = (out_ref[rows].astype(FULL) + (own.astype(FULL) + far.astype(FULL))).astype(LOW)

    total(slice(0, EDGE), part_ref[:EDGE], far_part_ref[:EDGE])
    total(slice(EDGE, inner), mid_ref[...], far_mid_ref[...])
    total(slice(inner, frames), part_ref[EDGE:], far_part_ref[EDGE:])
    rows = send_ref.shape[1]
    for out, flip in ((send_ref, 1), (keep_ref, 0)):
        for half in range(2):
            block = 2 * half + (1 - core if flip else core)
            span = pl.ds(pl.multiple_of(block * rows, rows), rows)
            out[half] = dot_tn(resid_ref[:, span], attended_ref[...]).astype(LOW)
    frame = lax.broadcasted_iota(jnp.int32, grad_ref.shape, 0) + first
    grad = dot_nt(resid_ref[...], weight_ref[...])
    grad_ref[...] = jnp.where(frame < length, grad, 0.0).astype(LOW)


def resid(place, out_rows, mid, far_mid, part, far_part, weight, attended):
    frames, wide = out_rows.shape
    cols = attended.shape[1]
    return call(
        resid_kernel, "resid",
        (place, out_rows, mid, far_mid, part, far_part, weight, attended),
        [SMEM] + [VMEM] * 7,
        [shape((frames, wide)), shape((frames, cols))] + [shape((2, wide // 4, cols))] * 2, micros=60,
    )


def by_peer(rows, peers):
    groups = rows.reshape(rows.shape[0] // (8 * peers), peers, 8, rows.shape[1])
    return [groups[:, peer].reshape(-1, rows.shape[1]) for peer in range(peers)]


def add_kernel(own_ref, arrived_ref, sum_ref):
    peers, share = sum_ref.shape[0], sum_ref.shape[1] // 2
    for half in range(2):
        total = own_ref[half].astype(FULL) + arrived_ref[half].astype(FULL)
        for peer, rows in enumerate(by_peer(total, peers)):
            sum_ref[peer, half * share : (half + 1) * share] = rows.astype(LOW)


def add(own, arrived, peers):
    halves, rows, cols = own.shape
    dims = (peers, halves * rows // peers, cols)
    return call(add_kernel, "add", (own, arrived), [VMEM, VMEM], [shape(dims)])[0]


def plane_kernel(*refs):
    *sources, sum_ref = refs
    at = 0
    for parts_ref in sources:
        for start in range(0, parts_ref.shape[2], 256):
            lanes = slice(start, start + 256)
            total = parts_ref[0, :, lanes].astype(FULL)
            for i in range(1, parts_ref.shape[0]):
                total = total + parts_ref[i, :, lanes].astype(FULL)
            sum_ref[:, at : at + 256] = total.astype(LOW)
            at += 256


def plane_sum(*parts):
    dims = (parts[0].shape[1], sum(part.shape[2] for part in parts))
    return call(plane_kernel, "plane_sum", parts, [VMEM] * len(parts), [shape(dims)])[0]


def line_kernel(parts_ref, out_ref, glu_ref, proj_ref):
    total = parts_ref[0].astype(FULL)
    for i in range(1, parts_ref.shape[0]):
        total = total + parts_ref[i].astype(FULL)
    cols = out_ref.shape[1]
    glu_ref[0] = total[:, :cols].astype(LOW)
    glu_ref[1] = total[:, cols : 2 * cols].astype(LOW)
    proj_ref[...] = total[:, 2 * cols : 3 * cols].astype(LOW)
    out_ref[...] = total[:, 3 * cols :].astype(LOW)


def line_sum(parts):
    rows, cols = parts.shape[1], parts.shape[2] // 4
    return call(
        line_kernel, "line_sum", (parts,), [VMEM], [shape((rows, cols)), shape((2, rows, cols)), shape((rows, cols))]
    )


def exchanged(parts, groups):
    return lax.all_to_all(parts, ("dp", "seq"), 0, 0, axis_index_groups=groups)


BLOCK = 128
CHUNK = 128
SPAN = BLOCK + 2 * WIN
SCALE = HEAD_DIM**-0.5
PAIR = 2 * HEAD_DIM


def side_by_side(rows):
    lane = lax.broadcasted_iota(jnp.int32, rows.shape, 1)
    zero = jnp.zeros_like(rows)
    return jnp.concatenate(
        [jnp.where(lane < HEAD_DIM, rows, zero), jnp.where(lane < HEAD_DIM, zero, rows)], axis=0
    )


def own_columns(columns):
    return jnp.concatenate([columns[:HEAD_DIM, :BLOCK], columns[HEAD_DIM:, BLOCK:]], axis=0)


def gather_rows(whole, before_ref, own_ref, after_ref):
    frames = own_ref.shape[0]
    whole[:WIN] = before_ref[...]
    whole[WIN : WIN + frames] = own_ref[...]
    whole[WIN + frames :] = after_ref[...]


def pair_specs(frames, pairs, start=0):
    own = pl.BlockSpec((frames, PAIR), lambda i: (0, i + start))
    far_key = pl.BlockSpec((WIN, PAIR), lambda i: (0, i + start))
    far_value = pl.BlockSpec((WIN, PAIR), lambda i: (0, i + start + pairs))
    return own, far_key, far_value


def attend_kernel(
    place, q_ref, k_ref, v_ref, kb_ref, vb_ref, ka_ref, va_ref,
    weight_ref, out_ref, share_ref, fill, scores, keys, values,
):
    first, length = place[0], place[1]
    frames = q_ref.shape[0]

    @pl.when(pl.program_id(0) == 0)
    def _():
        for block in range(frames // BLOCK):
            key = lax.broadcasted_iota(jnp.int32, (SPAN, BLOCK), 0)
            offset = key - lax.broadcasted_iota(jnp.int32, (SPAN, BLOCK), 1)
            frame = key + (first - WIN + block * BLOCK)
            allowed = (offset >= 0) & (offset <= 2 * WIN) & (frame >= 0) & (frame < length)
            fill[block] = jnp.where(allowed, 0.0, NEG_FILL)

    gather_rows(keys, kb_ref, k_ref, ka_ref)
    gather_rows(values, vb_ref, v_ref, va_ref)
    for block in range(frames // BLOCK):
        rows = slice(block * BLOCK, (block + 1) * BLOCK)
        start = block * BLOCK
        queries = side_by_side(q_ref[rows] * SCALE)
        top = jnp.full((8, 2 * BLOCK), NEG_FILL, FULL)
        for at in range(0, SPAN, CHUNK):
            part = dot_nt(keys[start + at : start + at + CHUNK], queries)
            bias = fill[block, at : at + CHUNK]
            part = part + jnp.concatenate([bias, bias], axis=1)
            scores[at : at + CHUNK] = part
            top = jnp.maximum(top, jnp.max(part.reshape(CHUNK // 8, 8, 2 * BLOCK), axis=0))
        top = jnp.max(top, axis=0, keepdims=True)
        total = jnp.zeros((8, 2 * BLOCK), FULL)
        for at in range(0, SPAN, CHUNK):
            part = jnp.exp(scores[at : at + CHUNK] - top)
            total = total + jnp.sum(part.reshape(CHUNK // 8, 8, 2 * BLOCK), axis=0)
            weight_ref[0, block, at : at + CHUNK] = part.astype(LOW)
        share = 1.0 / jnp.sum(total, axis=0, keepdims=True)
        summed = own_columns(dot_tn(values[start : start + SPAN], weight_ref[0, block]) * share)
        frame = lax.broadcasted_iota(jnp.int32, (1, BLOCK), 1) + (first + block * BLOCK)
        out_ref[rows] = jnp.where(frame < length, summed, 0.0).T.astype(LOW)
        share_ref[rows] = own_columns(jnp.broadcast_to(share, (PAIR, 2 * BLOCK))).T


def attend_grad_kernel(
    q_ref, k_ref, v_ref, kb_ref, vb_ref, ka_ref, va_ref, weight_ref, out_ref, share_ref, grad_ref, *refs
):
    dq_ref, dk_ref, dv_ref, to_before_ref, to_after_ref, keys, values, key_sum, value_sum = refs[-9:]
    frames = q_ref.shape[0]
    gather_rows(keys, kb_ref, k_ref, ka_ref)
    gather_rows(values, vb_ref, v_ref, va_ref)
    key_sum[...] = jnp.zeros_like(key_sum)
    value_sum[...] = jnp.zeros_like(value_sum)
    for block in range(frames // BLOCK):
        rows = slice(block * BLOCK, (block + 1) * BLOCK)
        span = slice(block * BLOCK, block * BLOCK + SPAN)
        queries = side_by_side(q_ref[rows] * SCALE)
        grad_rows = (grad_ref[rows].astype(FULL) * share_ref[rows]).astype(LOW)
        grads = side_by_side(grad_rows)
        product = (grad_rows.astype(FULL) * out_ref[rows].astype(FULL)).T
        row_delta = jnp.concatenate(
            [
                jnp.sum(product[:HEAD_DIM], axis=0, keepdims=True),
                jnp.sum(product[HEAD_DIM:], axis=0, keepdims=True),
            ],
            axis=1,
        )
        weight = weight_ref[0, block]
        grad_prob = dot_nt(values[span], grads)
        grad_score = (weight.astype(FULL) * (grad_prob - row_delta)).astype(LOW)
        value_sum[span] += jnp.dot(weight, grads, preferred_element_type=FULL)
        key_sum[span] += jnp.dot(grad_score, queries, preferred_element_type=FULL)
        grad_query = dot_tn(keys[span], grad_score)
        dq_ref[rows] = (own_columns(grad_query).T * SCALE).astype(LOW)
    for total, inner, lane in ((key_sum, dk_ref, 0), (value_sum, dv_ref, PAIR)):
        to_before_ref[:, lane : lane + PAIR] = total[:WIN].astype(LOW)
        inner[...] = total[WIN : WIN + frames]
        to_after_ref[:, lane : lane + PAIR] = total[WIN + frames :].astype(LOW)


def attend(place, q_rows, k_rows, v_rows, before, after):
    frames, cols = q_rows.shape
    pairs, blocks = cols // PAIR, frames // BLOCK
    own, far_key, far_value = pair_specs(frames, pairs)
    return call(
        attend_kernel, "attend", (place, q_rows, k_rows, v_rows, before, before, after, after),
        [SMEM, own, own, own, far_key, far_value, far_key, far_value],
        [shape((pairs, blocks, SPAN, 2 * BLOCK)), shape((frames, cols)), shape((frames, cols), FULL)],
        out_specs=[pl.BlockSpec((1, blocks, SPAN, 2 * BLOCK), lambda i: (i, 0, 0, 0)), own, own],
        scratch=[pltpu.VMEM((blocks, SPAN, BLOCK), FULL), pltpu.VMEM((SPAN, 2 * BLOCK), FULL)] + [pltpu.VMEM((frames + 2 * WIN, PAIR), LOW)] * 2,
        grid=(pairs,), micros=0.5, limit=57,
    )


def attend_grad(q_rows, k_rows, v_rows, before, after, weight, attended, share, grad_attn, start, count, earlier=()):
    frames, cols = q_rows.shape
    pairs, blocks = cols // PAIR, frames // BLOCK
    own, far_key, far_value = pair_specs(frames, pairs, start)
    far = pl.BlockSpec((WIN, 2 * PAIR), lambda i: (0, i + start))
    weights = pl.BlockSpec((1, blocks, SPAN, 2 * BLOCK), lambda i: (i + start, 0, 0, 0))
    return call(
        attend_grad_kernel, "attend_grad",
        (q_rows, k_rows, v_rows, before, before, after, after, weight, attended, share, grad_attn, *earlier),
        [own, own, own, far_key, far_value, far_key, far_value, weights, own, own, own] + [HBM] * len(earlier),
        [shape((frames, cols))] + [shape((frames, cols), FULL)] * 2 + [shape((WIN, 2 * cols))] * 2,
        out_specs=[own, own, own, far, far],
        scratch=[pltpu.VMEM((frames + 2 * WIN, PAIR), LOW)] * 2 + [pltpu.VMEM((frames + 2 * WIN, PAIR), FULL)] * 2,
        grid=(count,), micros=1, limit=58,
        input_output_aliases={11 + i: i for i in range(len(earlier))},
    )


def finish_kernel(dk_ref, dv_ref, from_before_ref, from_after_ref, key_ref, value_ref):
    frames, cols = dk_ref.shape
    shared = frames - WIN
    for own, out, lane in ((dk_ref, key_ref, 0), (dv_ref, value_ref, PAIR)):
        for start in range(0, cols, PAIR):
            span = slice(start, start + PAIR)
            far_span = slice(2 * start + lane, 2 * start + lane + PAIR)
            above = own[:WIN, span] + from_before_ref[:, far_span].astype(FULL)
            far = from_after_ref[:, far_span].astype(FULL)
            out[:shared, span] = above[:shared].astype(LOW)
            out[shared:WIN, span] = (above[shared:] + far[: WIN - shared]).astype(LOW)
            out[WIN:, span] = (own[WIN:, span] + far[WIN - shared :]).astype(LOW)


def finish(grad_key, grad_value, from_before, from_after):
    own = pl.BlockSpec(grad_key.shape, lambda i: (0, 0))
    far = pl.BlockSpec(from_before.shape, lambda i: (0, 0))
    return call(
        finish_kernel, "finish", (grad_key, grad_value, from_before, from_after), [own, own, far, far],
        [shape(grad_key.shape)] * 2, out_specs=[own, own], grid=(1,), micros=2, limit=58,
    )


def local(
    lengths,
    query_act,
    key_act,
    value_act,
    conv_input,
    conv_result,
    out_grad,
    out_weight,
    glu_weight,
    conv_taps,
    proj_weight,
):
    q_rows, k_rows, v_rows = (query_act[0], key_act[0], value_act[0])
    input_rows, pre_rows, out_rows = (conv_input[0], conv_result[0], out_grad[0])
    frames, cols = q_rows.shape
    peers = lax.axis_size("seq")
    index = lax.axis_index("dp")
    first = lax.axis_index("seq") * frames
    place = jnp.stack([first, lengths[0], peers * frames, index % 2, index // 2]).astype(jnp.int32)

    up, down = pack(k_rows, v_rows, out_rows, pre_rows)
    before, after = (round_ring(up, 1), round_ring(down, -1))
    mid, glu_low, activated, rim_rows, rim_gate, rim_value = front(
        place, out_rows, pre_rows, proj_weight, input_rows, glu_weight, conv_taps
    )
    far_mid = swapped(mid, "tensor", 1)
    part, glu_low = rim(
        place, before, after, rim_rows, rim_gate, rim_value, proj_weight, glu_weight, conv_taps, glu_low
    )
    far_part = swapped(part, "tensor", 1)
    given = [swapped(term, "dp", 1) for term in terms(place, input_rows, glu_low, out_rows, activated)]
    on_chip = terms(place, input_rows, glu_low, out_rows, activated, given)[0]
    q_late, on_chip = lax.optimization_barrier((q_rows, on_chip))
    weight, attended, share = attend(place, q_late, k_rows, v_rows, before, after)
    resid_low, grad_attn, out_send, out_keep = resid(
        place, out_rows, mid, far_mid, part, far_part, out_weight, attended
    )
    near, far = (8, peers // 8)
    by_plane = [[d * peers + z * near + i for i in range(near)] for d in range(4) for z in range(far)]
    by_line = [
        [(2 * y + core) * peers + z * near + i for y in range(2) for z in range(far)]
        for core in range(2) for i in range(near)
    ]
    rest = exchanged(on_chip, by_plane)
    operands = (q_rows, k_rows, v_rows, before, after, weight, attended, share, grad_attn)
    early = attend_grad(*operands, 0, 1)
    out_given, early = lax.optimization_barrier((swapped(out_send, "dp", 1), early))
    on_chip_out = add(out_keep, out_given, near)
    grad_query, grad_key, grad_value, to_before, to_after = attend_grad(*operands, 1, 3, early)
    from_after, from_before = (round_ring(to_before, -1), round_ring(to_after, 1))
    on_chip_out, rest = lax.optimization_barrier((on_chip_out, rest))
    plane = plane_sum(rest, exchanged(on_chip_out, by_plane))
    out_sum, glu_sum, proj_sum = line_sum(exchanged(plane.reshape(2 * far, -1, plane.shape[1]), by_line))
    key_grad, value_grad = finish(grad_key, grad_value, from_before, from_after)
    return (
        resid_low[None],
        grad_query[None],
        key_grad[None],
        value_grad[None],
        out_sum.T,
        glu_sum,
        proj_sum.T,
    )


def solution(mesh):
    in_specs = (
        P("dp"),
        P("dp", "seq", "tensor"),
        P("dp", "seq", "tensor"),
        P("dp", "seq", "tensor"),
        P("dp", "seq", None),
        P("dp", "seq", "tensor"),
        P("dp", "seq", None),
        P("tensor", None),
        P(None, None, "tensor"),
        P(None, "tensor"),
        P("tensor", None),
    )
    out_specs = (
        P("dp", "seq", None),
        P("dp", "seq", "tensor"),
        P("dp", "seq", "tensor"),
        P("dp", "seq", "tensor"),
        P("tensor", ("dp", "seq")),
        P(None, ("dp", "seq"), "tensor"),
        P("tensor", ("dp", "seq")),
    )
    return jax.shard_map(local, mesh=mesh, in_specs=in_specs, out_specs=out_specs, check_vma=False)
```

```python
import functools

import jax
import jax.numpy as jnp
from jax import lax
from jax.experimental import pallas as pl
from jax.experimental.pallas import tpu as pltpu
from jax.sharding import PartitionSpec as P

HEAD_DIM = 64
WIN = 256


NEG_FILL = -1e30
FULL, LOW = jnp.float32, jnp.bfloat16
TAPS = 31
EDGE = 16
STRIP = 32
VMEM = pl.BlockSpec(memory_space=pltpu.VMEM)
SMEM = pl.BlockSpec(memory_space=pltpu.SMEM)
HBM = pl.BlockSpec(memory_space=pltpu.HBM)


def shape(dims, kind=LOW):
    return jax.ShapeDtypeStruct(dims, kind)


def call(kernel, name, operands, in_specs, out_shape, out_specs=None, scratch=(), micros=1, limit=24, **more):
    return pl.pallas_call(
        kernel,
        in_specs=in_specs,
        out_specs=[VMEM] * len(out_shape) if out_specs is None else out_specs,
        out_shape=out_shape,
        scratch_shapes=list(scratch),
        compiler_params=pltpu.CompilerParams(vmem_limit_bytes=limit * 2**20),
        cost_estimate=pl.CostEstimate(flops=int(micros * 9e8), bytes_accessed=1, transcendentals=0),
        name=name,
        **more,
    )(*operands)


def whole(array):
    return pl.BlockSpec(array.shape, lambda i: (0,) * array.ndim)


def dot_nt(left, right):
    return lax.dot_general(left, right, (((1,), (1,)), ((), ())), preferred_element_type=FULL)


def dot_tn(left, right):
    return lax.dot_general(left, right, (((0,), (0,)), ((), ())), preferred_element_type=FULL)


def round_ring(value, steps):
    count = lax.axis_size("seq")
    return lax.ppermute(value, "seq", [(i, (i + steps) % count) for i in range(count)])


def swapped(value, axis, stride):
    count = lax.axis_size(axis)
    return lax.ppermute(value, axis, [(i, i ^ stride) for i in range(count)])


def pack_kernel(k_ref, v_ref, grad_ref, pre_ref, up_ref, down_ref, sems):
    frames, cols = k_ref.shape
    copies = []
    for out_ref, start, edge in ((up_ref, frames - WIN, frames - EDGE), (down_ref, 0, 0)):
        for source, rows, count, first, span in (
            (k_ref, 0, WIN, start, slice(0, cols)),
            (v_ref, 0, WIN, start, slice(cols, 2 * cols)),
            (grad_ref, WIN, EDGE, edge, slice(0, 2 * cols)),
            (pre_ref, WIN + EDGE, EDGE, edge, slice(0, cols)),
        ):
            copies.append(
                pltpu.make_async_copy(
                    source.at[pl.ds(first, count)], out_ref.at[pl.ds(rows, count), span], sems.at[len(copies)]
                )
            )
    for copy in copies:
        copy.start()
    for out_ref in (up_ref, down_ref):
        out_ref[WIN + EDGE :, cols:] = jnp.zeros((EDGE, cols), LOW)
    for copy in copies:
        copy.wait()


def pack(k_rows, v_rows, out_rows, pre_rows):
    dims = (WIN + 2 * EDGE, 2 * k_rows.shape[1])
    return call(
        pack_kernel, "pack", (k_rows, v_rows, out_rows, pre_rows), [HBM] * 4, [shape(dims)] * 2,
        scratch=[pltpu.SemaphoreType.DMA((8,))], limit=58,
    )


def pre_grad(out_rows, pre_rows, proj):
    pre = pre_rows.astype(FULL)
    logistic = jax.nn.sigmoid(pre)
    slope = logistic * (1.0 + pre * (1.0 - logistic))
    return (dot_nt(out_rows, proj) * slope).astype(LOW), (pre * logistic).astype(LOW)


def conv_strip(rows, taps):
    count = rows.shape[0] - 2 * EDGE
    total = jnp.zeros((count, rows.shape[1]), FULL)
    for shift in range(8):
        moved = rows[shift : shift + count + 24]
        for coarse in range(4):
            step = 8 * coarse + shift
            if step >= 1:
                total = total + taps[TAPS - step : TAPS - step + 1] * moved[8 * coarse : 8 * coarse + count]
    return total


def glu_grads(grad_conv, logistic, value):
    first = grad_conv * logistic
    return first.astype(LOW), (first * value * (1.0 - logistic)).astype(LOW)


def front_kernel(
    place, out_ref, pre_ref, proj_ref, input_ref, glu_w_ref, taps_ref,
    mid_ref, glu_ref, act_ref, rim_ref, rim_gate_ref, rim_value_ref,
    padded, taps, gates, values,
):
    frames, cols = pre_ref.shape
    first, length = place[0], place[1]
    inner = frames - EDGE
    taps[:TAPS] = taps_ref[...].astype(FULL)
    for part in range(0, cols, 256):
        span = slice(part, part + 256)
        grad_act = dot_nt(out_ref[...], proj_ref[span])
        for at in range(0, frames, 64):
            rows = slice(at, at + 64)
            pre = pre_ref[rows, span].astype(FULL)
            logistic = jax.nn.sigmoid(pre)
            slope = logistic * (1.0 + pre * (1.0 - logistic))
            padded[rows, span] = (grad_act[rows] * slope).astype(LOW).astype(FULL)
            act_ref[rows, span] = (pre * logistic).astype(LOW)
        rim_ref[: 2 * EDGE, span] = padded[: 2 * EDGE, span].astype(LOW)
        rim_ref[2 * EDGE :, span] = padded[frames - 2 * EDGE :, span].astype(LOW)
        values[:, span] = jnp.dot(input_ref[...], glu_w_ref[0, :, span], preferred_element_type=FULL)
        gate_half = jnp.dot(input_ref[...], glu_w_ref[1, :, span], preferred_element_type=FULL)
        for at in range(0, frames, 64):
            gates[at : at + 64, span] = jax.nn.sigmoid(gate_half[at : at + 64])
    for whole, rim in ((gates, rim_gate_ref), (values, rim_value_ref)):
        rim[:EDGE] = whole[:EDGE]
        rim[EDGE:] = whole[inner:]

    def strip(i, carry):
        at = pl.multiple_of(i * STRIP, STRIP)
        rows = pl.ds(pl.multiple_of(at + EDGE, EDGE), STRIP)
        frame = lax.broadcasted_iota(jnp.int32, (STRIP, 128), 0) + (first + EDGE + at)
        valid = frame < length
        for part in range(0, cols, 128):
            span = slice(part, part + 128)
            grad_conv = conv_strip(padded[pl.ds(at, STRIP + 2 * EDGE), span], taps[:, span])
            grad_conv = jnp.where(valid, grad_conv, 0.0)
            low = glu_grads(grad_conv, gates[rows, span], values[rows, span])
            glu_ref[rows, span] = low[0]
            glu_ref[rows, cols + part : cols + part + 128] = low[1]
        return carry

    lax.fori_loop(0, (frames - 2 * EDGE) // STRIP, strip, 0)
    for part in range(0, mid_ref.shape[1], 256):
        span = slice(part, part + 256)
        mid_ref[:, span] = (
            dot_nt(glu_ref[EDGE:inner, :cols], glu_w_ref[0, span])
            + dot_nt(glu_ref[EDGE:inner, cols:], glu_w_ref[1, span])
        ).astype(LOW)


def front(place, out_rows, pre_rows, proj, input_rows, glu_weight, taps):
    frames, cols = pre_rows.shape
    wide = input_rows.shape[1]
    return call(
        front_kernel, "front",
        (place, out_rows, pre_rows, proj, input_rows, glu_weight, taps),
        [SMEM] + [VMEM] * 6,
        [
            shape((frames - 2 * EDGE, wide)), shape((frames, 2 * cols)), shape((frames, cols)),
            shape((4 * EDGE, cols)), shape((2 * EDGE, cols), FULL), shape((2 * EDGE, cols), FULL),
        ],
        scratch=[
            pltpu.VMEM((frames, cols), FULL), pltpu.VMEM((32, cols), FULL),
            pltpu.VMEM((frames, cols), FULL), pltpu.VMEM((frames, cols), FULL),
        ],
        micros=7,
    )


def rim_kernel(
    place, before_ref, after_ref, rim_ref, gate_ref, value_ref, proj_ref, glu_w_ref, taps_ref, glu_in_ref,
    part_ref, glu_ref,
):
    frames = glu_ref.shape[0]
    cols = rim_ref.shape[1]
    first, length, total = place[0], place[1], place[2]
    del glu_in_ref
    out_rows = jnp.concatenate([before_ref[:EDGE], after_ref[:EDGE]], axis=0)
    pre_rows = jnp.concatenate([before_ref[EDGE:, :cols], after_ref[EDGE:, :cols]], axis=0)
    arrived = pre_grad(out_rows, pre_rows, proj_ref[...])[0].astype(FULL)
    above = jnp.where(first > 0, arrived[:EDGE], 0.0)
    below = jnp.where(first + frames < total, arrived[EDGE:], 0.0)
    own = rim_ref[...].astype(FULL)
    taps = taps_ref[...].astype(FULL)
    pieces = []
    for rows, start, place_of in (
        (jnp.concatenate([above, own[: 2 * EDGE]], axis=0), 0, slice(0, EDGE)),
        (jnp.concatenate([own[2 * EDGE :], below], axis=0), frames - EDGE, slice(EDGE, 2 * EDGE)),
    ):
        lows = []
        for part in range(0, cols, 128):
            span = slice(part, part + 128)
            frame = lax.broadcasted_iota(jnp.int32, (EDGE, 128), 0) + (first + start)
            grad_conv = jnp.where(frame < length, conv_strip(rows[:, span], taps[:, span]), 0.0)
            lows.append(glu_grads(grad_conv, gate_ref[place_of, span], value_ref[place_of, span]))
        low = jnp.concatenate([pair[0] for pair in lows] + [pair[1] for pair in lows], axis=1)
        glu_ref[start : start + EDGE] = low
        pieces.append(low)
    low = jnp.concatenate(pieces, axis=0)
    part_ref[...] = (dot_nt(low[:, :cols], glu_w_ref[0]) + dot_nt(low[:, cols:], glu_w_ref[1])).astype(LOW)


def rim(place, before, after, rim_rows, gate, value, proj, glu_weight, taps, glu_low):
    edge = pl.BlockSpec((2 * EDGE, before.shape[1]), lambda i: (WIN // (2 * EDGE), 0))
    wide = glu_weight.shape[1]
    return call(
        rim_kernel, "rim",
        (place, before, after, rim_rows, gate, value, proj, glu_weight, taps, glu_low),
        [SMEM, edge, edge, whole(rim_rows), whole(gate), whole(value), VMEM, VMEM, whole(taps), VMEM],
        [shape((2 * EDGE, wide)), shape(glu_low.shape)],
        out_specs=[pl.BlockSpec((2 * EDGE, wide), lambda i: (0, 0)), VMEM],
        grid=(1,), micros=0.1, input_output_aliases={9: 1},
    )


def terms_kernel(keeps, place, input_ref, glu_ref, out_ref, act_ref, *refs):
    core = place[3]
    cols = act_ref.shape[1]
    rows = input_ref.shape[1] // 4
    peers = 8
    share = rows // peers
    sources = ((input_ref, glu_ref, 0), (input_ref, glu_ref, cols), (out_ref, act_ref, 0))
    leaving = []
    for which, (source, low, start) in enumerate(sources):
        for half in range(2):
            block = 2 * half + (core if keeps else 1 - core)
            left = source[:, pl.ds(pl.multiple_of(block * rows, rows), rows)]
            for part in range(0, cols, 256):
                term = dot_tn(left, low[:, start + part : start + part + 256])
                at = slice(part, part + 256)
                if not keeps:
                    refs[which][half, :, at] = term.astype(LOW)
                    continue
                term = term + refs[which][half, :, at].astype(FULL)
                at = slice(cols * which + part, cols * which + part + 256)
                for peer, moved in enumerate(by_peer(term, peers)):
                    refs[4][peer, half * share : (half + 1) * share, at] = moved.astype(LOW)
        if keeps:
            at = slice(cols * which, cols * which + cols)
            leaving.append(pltpu.make_async_copy(refs[4].at[:, :, at], refs[3].at[:, :, at], refs[5].at[which]))
            leaving[-1].start()
    for copy in leaving:
        copy.wait()


def terms(place, input_rows, glu_low, out_rows, activated, arrived=()):
    wide, cols = input_rows.shape[1], activated.shape[1]
    operands = (place, input_rows, glu_low, out_rows, activated) + tuple(arrived)
    joined = (8, wide // 16, 3 * cols)
    if arrived:
        more = dict(out_specs=[HBM], scratch=[pltpu.VMEM(joined, LOW), pltpu.SemaphoreType.DMA((3,))])
    else:
        more = {}
    return call(
        functools.partial(terms_kernel, bool(arrived)), "terms",
        operands, [SMEM] + [VMEM] * (len(operands) - 1),
        [shape(joined)] if arrived else [shape((2, wide // 4, cols))] * 3, micros=0.1, **more,
    )


def resid_kernel(
    place, out_ref, mid_ref, far_mid_ref, part_ref, far_part_ref, weight_ref, attended_ref,
    resid_ref, grad_ref, send_ref, keep_ref,
):
    frames = out_ref.shape[0]
    first, length, core = place[0], place[1], place[3]
    inner = frames - EDGE

    def total(rows, own, far):
        resid_ref[rows] = (out_ref[rows].astype(FULL) + (own.astype(FULL) + far.astype(FULL))).astype(LOW)

    total(slice(0, EDGE), part_ref[:EDGE], far_part_ref[:EDGE])
    total(slice(EDGE, inner), mid_ref[...], far_mid_ref[...])
    total(slice(inner, frames), part_ref[EDGE:], far_part_ref[EDGE:])
    rows = send_ref.shape[1]
    for out, flip in ((send_ref, 1), (keep_ref, 0)):
        for half in range(2):
            block = 2 * half + (1 - core if flip else core)
            span = pl.ds(pl.multiple_of(block * rows, rows), rows)
            out[half] = dot_tn(resid_ref[:, span], attended_ref[...]).astype(LOW)
    frame = lax.broadcasted_iota(jnp.int32, grad_ref.shape, 0) + first
    grad = dot_nt(resid_ref[...], weight_ref[...])
    grad_ref[...] = jnp.where(frame < length, grad, 0.0).astype(LOW)


def resid(place, out_rows, mid, far_mid, part, far_part, weight, attended):
    frames, wide = out_rows.shape
    cols = attended.shape[1]
    return call(
        resid_kernel, "resid",
        (place, out_rows, mid, far_mid, part, far_part, weight, attended),
        [SMEM] + [VMEM] * 7,
        [shape((frames, wide)), shape((frames, cols))] + [shape((2, wide // 4, cols))] * 2, micros=60,
    )


def by_peer(rows, peers):
    groups = rows.reshape(rows.shape[0] // (8 * peers), peers, 8, rows.shape[1])
    return [groups[:, peer].reshape(-1, rows.shape[1]) for peer in range(peers)]


def add_kernel(own_ref, arrived_ref, sum_ref):
    peers, share = sum_ref.shape[0], sum_ref.shape[1] // 2
    for half in range(2):
        total = own_ref[half].astype(FULL) + arrived_ref[half].astype(FULL)
        for peer, rows in enumerate(by_peer(total, peers)):
            sum_ref[peer, half * share : (half + 1) * share] = rows.astype(LOW)


def add(own, arrived, peers):
    halves, rows, cols = own.shape
    dims = (peers, halves * rows // peers, cols)
    return call(add_kernel, "add", (own, arrived), [VMEM, VMEM], [shape(dims)])[0]


def plane_kernel(*refs):
    *sources, sum_ref = refs
    at = 0
    for parts_ref in sources:
        for start in range(0, parts_ref.shape[2], 256):
            lanes = slice(start, start + 256)
            total = parts_ref[0, :, lanes].astype(FULL)
            for i in range(1, parts_ref.shape[0]):
                total = total + parts_ref[i, :, lanes].astype(FULL)
            sum_ref[:, at : at + 256] = total.astype(LOW)
            at += 256


def plane_sum(*parts):
    dims = (parts[0].shape[1], sum(part.shape[2] for part in parts))
    return call(plane_kernel, "plane_sum", parts, [VMEM] * len(parts), [shape(dims)])[0]


def line_kernel(parts_ref, out_ref, glu_ref, proj_ref):
    total = parts_ref[0].astype(FULL)
    for i in range(1, parts_ref.shape[0]):
        total = total + parts_ref[i].astype(FULL)
    cols = out_ref.shape[1]
    glu_ref[0] = total[:, :cols].astype(LOW)
    glu_ref[1] = total[:, cols : 2 * cols].astype(LOW)
    proj_ref[...] = total[:, 2 * cols : 3 * cols].astype(LOW)
    out_ref[...] = total[:, 3 * cols :].astype(LOW)


def line_sum(parts):
    rows, cols = parts.shape[1], parts.shape[2] // 4
    return call(
        line_kernel, "line_sum", (parts,), [VMEM], [shape((rows, cols)), shape((2, rows, cols)), shape((rows, cols))]
    )


def exchanged(parts, groups):
    return lax.all_to_all(parts, ("dp", "seq"), 0, 0, axis_index_groups=groups)


BLOCK = 128
CHUNK = 128
SPAN = BLOCK + 2 * WIN
SCALE = HEAD_DIM**-0.5
PAIR = 2 * HEAD_DIM


def side_by_side(rows):
    lane = lax.broadcasted_iota(jnp.int32, rows.shape, 1)
    zero = jnp.zeros_like(rows)
    return jnp.concatenate(
        [jnp.where(lane < HEAD_DIM, rows, zero), jnp.where(lane < HEAD_DIM, zero, rows)], axis=0
    )


def own_columns(columns):
    return jnp.concatenate([columns[:HEAD_DIM, :BLOCK], columns[HEAD_DIM:, BLOCK:]], axis=0)


def gather_rows(whole, before_ref, own_ref, after_ref):
    frames = own_ref.shape[0]
    whole[:WIN] = before_ref[...]
    whole[WIN : WIN + frames] = own_ref[...]
    whole[WIN + frames :] = after_ref[...]


def pair_specs(frames, pairs, start=0):
    own = pl.BlockSpec((frames, PAIR), lambda i: (0, i + start))
    far_key = pl.BlockSpec((WIN, PAIR), lambda i: (0, i + start))
    far_value = pl.BlockSpec((WIN, PAIR), lambda i: (0, i + start + pairs))
    return own, far_key, far_value


def attend_kernel(
    place, q_ref, k_ref, v_ref, kb_ref, vb_ref, ka_ref, va_ref,
    weight_ref, out_ref, share_ref, fill, scores, keys, values,
):
    first, length = place[0], place[1]
    frames = q_ref.shape[0]

    @pl.when(pl.program_id(0) == 0)
    def _():
        for block in range(frames // BLOCK):
            key = lax.broadcasted_iota(jnp.int32, (SPAN, BLOCK), 0)
            offset = key - lax.broadcasted_iota(jnp.int32, (SPAN, BLOCK), 1)
            frame = key + (first - WIN + block * BLOCK)
            allowed = (offset >= 0) & (offset <= 2 * WIN) & (frame >= 0) & (frame < length)
            fill[block] = jnp.where(allowed, 0.0, NEG_FILL)

    gather_rows(keys, kb_ref, k_ref, ka_ref)
    gather_rows(values, vb_ref, v_ref, va_ref)
    for block in range(frames // BLOCK):
        rows = slice(block * BLOCK, (block + 1) * BLOCK)
        start = block * BLOCK
        queries = side_by_side(q_ref[rows] * SCALE)
        top = jnp.full((8, 2 * BLOCK), NEG_FILL, FULL)
        for at in range(0, SPAN, CHUNK):
            part = dot_nt(keys[start + at : start + at + CHUNK], queries)
            bias = fill[block, at : at + CHUNK]
            part = part + jnp.concatenate([bias, bias], axis=1)
            scores[at : at + CHUNK] = part
            top = jnp.maximum(top, jnp.max(part.reshape(CHUNK // 8, 8, 2 * BLOCK), axis=0))
        top = jnp.max(top, axis=0, keepdims=True)
        total = jnp.zeros((8, 2 * BLOCK), FULL)
        for at in range(0, SPAN, CHUNK):
            part = jnp.exp(scores[at : at + CHUNK] - top)
            total = total + jnp.sum(part.reshape(CHUNK // 8, 8, 2 * BLOCK), axis=0)
            weight_ref[0, block, at : at + CHUNK] = part.astype(LOW)
        share = 1.0 / jnp.sum(total, axis=0, keepdims=True)
        summed = own_columns(dot_tn(values[start : start + SPAN], weight_ref[0, block]) * share)
        frame = lax.broadcasted_iota(jnp.int32, (1, BLOCK), 1) + (first + block * BLOCK)
        out_ref[rows] = jnp.where(frame < length, summed, 0.0).T.astype(LOW)
        share_ref[rows] = own_columns(jnp.broadcast_to(share, (PAIR, 2 * BLOCK))).T


def attend_grad_kernel(
    q_ref, k_ref, v_ref, kb_ref, vb_ref, ka_ref, va_ref, weight_ref, out_ref, share_ref, grad_ref, *refs
):
    dq_ref, dk_ref, dv_ref, to_before_ref, to_after_ref, keys, values, key_sum, value_sum = refs[-9:]
    frames = q_ref.shape[0]
    gather_rows(keys, kb_ref, k_ref, ka_ref)
    gather_rows(values, vb_ref, v_ref, va_ref)
    key_sum[...] = jnp.zeros_like(key_sum)
    value_sum[...] = jnp.zeros_like(value_sum)
    for block in range(frames // BLOCK):
        rows = slice(block * BLOCK, (block + 1) * BLOCK)
        span = slice(block * BLOCK, block * BLOCK + SPAN)
        queries = side_by_side(q_ref[rows] * SCALE)
        grad_rows = (grad_ref[rows].astype(FULL) * share_ref[rows]).astype(LOW)
        grads = side_by_side(grad_rows)
        product = (grad_rows.astype(FULL) * out_ref[rows].astype(FULL)).T
        row_delta = jnp.concatenate(
            [
                jnp.sum(product[:HEAD_DIM], axis=0, keepdims=True),
                jnp.sum(product[HEAD_DIM:], axis=0, keepdims=True),
            ],
            axis=1,
        )
        weight = weight_ref[0, block]
        grad_prob = dot_nt(values[span], grads)
        grad_score = (weight.astype(FULL) * (grad_prob - row_delta)).astype(LOW)
        value_sum[span] += jnp.dot(weight, grads, preferred_element_type=FULL)
        key_sum[span] += jnp.dot(grad_score, queries, preferred_element_type=FULL)
        grad_query = dot_tn(keys[span], grad_score)
        dq_ref[rows] = (own_columns(grad_query).T * SCALE).astype(LOW)
    for total, inner, lane in ((key_sum, dk_ref, 0), (value_sum, dv_ref, PAIR)):
        to_before_ref[:, lane : lane + PAIR] = total[:WIN].astype(LOW)
        inner[...] = total[WIN : WIN + frames]
        to_after_ref[:, lane : lane + PAIR] = total[WIN + frames :].astype(LOW)


def attend(place, q_rows, k_rows, v_rows, before, after):
    frames, cols = q_rows.shape
    pairs, blocks = cols // PAIR, frames // BLOCK
    own, far_key, far_value = pair_specs(frames, pairs)
    return call(
        attend_kernel, "attend", (place, q_rows, k_rows, v_rows, before, before, after, after),
        [SMEM, own, own, own, far_key, far_value, far_key, far_value],
        [shape((pairs, blocks, SPAN, 2 * BLOCK)), shape((frames, cols)), shape((frames, cols), FULL)],
        out_specs=[pl.BlockSpec((1, blocks, SPAN, 2 * BLOCK), lambda i: (i, 0, 0, 0)), own, own],
        scratch=[pltpu.VMEM((blocks, SPAN, BLOCK), FULL), pltpu.VMEM((SPAN, 2 * BLOCK), FULL)] + [pltpu.VMEM((frames + 2 * WIN, PAIR), LOW)] * 2,
        grid=(pairs,), micros=0.5, limit=57,
    )


def attend_grad(q_rows, k_rows, v_rows, before, after, weight, attended, share, grad_attn, start, count, earlier=()):
    frames, cols = q_rows.shape
    pairs, blocks = cols // PAIR, frames // BLOCK
    own, far_key, far_value = pair_specs(frames, pairs, start)
    far = pl.BlockSpec((WIN, 2 * PAIR), lambda i: (0, i + start))
    weights = pl.BlockSpec((1, blocks, SPAN, 2 * BLOCK), lambda i: (i + start, 0, 0, 0))
    return call(
        attend_grad_kernel, "attend_grad",
        (q_rows, k_rows, v_rows, before, before, after, after, weight, attended, share, grad_attn, *earlier),
        [own, own, own, far_key, far_value, far_key, far_value, weights, own, own, own] + [HBM] * len(earlier),
        [shape((frames, cols))] + [shape((frames, cols), FULL)] * 2 + [shape((WIN, 2 * cols))] * 2,
        out_specs=[own, own, own, far, far],
        scratch=[pltpu.VMEM((frames + 2 * WIN, PAIR), LOW)] * 2 + [pltpu.VMEM((frames + 2 * WIN, PAIR), FULL)] * 2,
        grid=(count,), micros=1, limit=58,
        input_output_aliases={11 + i: i for i in range(len(earlier))},
    )


def finish_kernel(dk_ref, dv_ref, from_before_ref, from_after_ref, key_ref, value_ref):
    frames, cols = dk_ref.shape
    shared = frames - WIN
    for own, out, lane in ((dk_ref, key_ref, 0), (dv_ref, value_ref, PAIR)):
        for start in range(0, cols, PAIR):
            span = slice(start, start + PAIR)
            far_span = slice(2 * start + lane, 2 * start + lane + PAIR)
            above = own[:WIN, span] + from_before_ref[:, far_span].astype(FULL)
            far = from_after_ref[:, far_span].astype(FULL)
            out[:shared, span] = above[:shared].astype(LOW)
            out[shared:WIN, span] = (above[shared:] + far[: WIN - shared]).astype(LOW)
            out[WIN:, span] = (own[WIN:, span] + far[WIN - shared :]).astype(LOW)


def finish(grad_key, grad_value, from_before, from_after):
    steps = 2
    own = pl.BlockSpec((grad_key.shape[0], grad_key.shape[1] // steps), lambda i: (0, i))
    far = pl.BlockSpec((from_before.shape[0], from_before.shape[1] // steps), lambda i: (0, i))
    return call(
        finish_kernel, "finish", (grad_key, grad_value, from_before, from_after), [own, own, far, far],
        [shape(grad_key.shape)] * 2, out_specs=[own, own], grid=(steps,), micros=2, limit=50,
    )


def local(
    lengths,
    query_act,
    key_act,
    value_act,
    conv_input,
    conv_result,
    out_grad,
    out_weight,
    glu_weight,
    conv_taps,
    proj_weight,
):
    q_rows, k_rows, v_rows = (query_act[0], key_act[0], value_act[0])
    input_rows, pre_rows, out_rows = (conv_input[0], conv_result[0], out_grad[0])
    frames, cols = q_rows.shape
    peers = lax.axis_size("seq")
    index = lax.axis_index("dp")
    first = lax.axis_index("seq") * frames
    place = jnp.stack([first, lengths[0], peers * frames, index % 2, index // 2]).astype(jnp.int32)

    up, down = pack(k_rows, v_rows, out_rows, pre_rows)
    before, after = (round_ring(up, 1), round_ring(down, -1))
    mid, glu_low, activated, rim_rows, rim_gate, rim_value = front(
        place, out_rows, pre_rows, proj_weight, input_rows, glu_weight, conv_taps
    )
    far_mid = swapped(mid, "tensor", 1)
    part, glu_low = rim(
        place, before, after, rim_rows, rim_gate, rim_value, proj_weight, glu_weight, conv_taps, glu_low
    )
    far_part = swapped(part, "tensor", 1)
    given = [swapped(term, "dp", 1) for term in terms(place, input_rows, glu_low, out_rows, activated)]
    on_chip = terms(place, input_rows, glu_low, out_rows, activated, given)[0]
    q_late, on_chip = lax.optimization_barrier((q_rows, on_chip))
    weight, attended, share = attend(place, q_late, k_rows, v_rows, before, after)
    resid_low, grad_attn, out_send, out_keep = resid(
        place, out_rows, mid, far_mid, part, far_part, out_weight, attended
    )
    near, far = (8, peers // 8)
    by_plane = [[d * peers + z * near + i for i in range(near)] for d in range(4) for z in range(far)]
    by_line = [
        [(2 * y + core) * peers + z * near + i for y in range(2) for z in range(far)]
        for core in range(2) for i in range(near)
    ]
    rest = exchanged(on_chip, by_plane)
    operands = (q_rows, k_rows, v_rows, before, after, weight, attended, share, grad_attn)
    early = attend_grad(*operands, 0, 2)
    out_given, early = lax.optimization_barrier((swapped(out_send, "dp", 1), early))
    on_chip_out = add(out_keep, out_given, near)
    grad_query, grad_key, grad_value, to_before, to_after = attend_grad(*operands, 2, 2, early)
    from_after, from_before = (round_ring(to_before, -1), round_ring(to_after, 1))
    on_chip_out, rest = lax.optimization_barrier((on_chip_out, rest))
    plane = plane_sum(rest, exchanged(on_chip_out, by_plane))
    out_sum, glu_sum, proj_sum = line_sum(exchanged(plane.reshape(2 * far, -1, plane.shape[1]), by_line))
    key_grad, value_grad = finish(grad_key, grad_value, from_before, from_after)
    return (
        resid_low[None],
        grad_query[None],
        key_grad[None],
        value_grad[None],
        out_sum.T,
        glu_sum,
        proj_sum.T,
    )


def solution(mesh):
    in_specs = (
        P("dp"),
        P("dp", "seq", "tensor"),
        P("dp", "seq", "tensor"),
        P("dp", "seq", "tensor"),
        P("dp", "seq", None),
        P("dp", "seq", "tensor"),
        P("dp", "seq", None),
        P("tensor", None),
        P(None, None, "tensor"),
        P(None, "tensor"),
        P("tensor", None),
    )
    out_specs = (
        P("dp", "seq", None),
        P("dp", "seq", "tensor"),
        P("dp", "seq", "tensor"),
        P("dp", "seq", "tensor"),
        P("tensor", ("dp", "seq")),
        P(None, ("dp", "seq"), "tensor"),
        P("tensor", ("dp", "seq")),
    )
    return jax.shard_map(local, mesh=mesh, in_specs=in_specs, out_specs=out_specs, check_vma=False)
```

```python
import functools

import jax
import jax.numpy as jnp
from jax import lax
from jax.experimental import pallas as pl
from jax.experimental.pallas import tpu as pltpu
from jax.sharding import PartitionSpec as P

HEAD_DIM = 64
WIN = 256


NEG_FILL = -1e30
FULL, LOW = jnp.float32, jnp.bfloat16
TAPS = 31
EDGE = 16
STRIP = 32
VMEM = pl.BlockSpec(memory_space=pltpu.VMEM)
SMEM = pl.BlockSpec(memory_space=pltpu.SMEM)
HBM = pl.BlockSpec(memory_space=pltpu.HBM)


def shape(dims, kind=LOW):
    return jax.ShapeDtypeStruct(dims, kind)


def call(kernel, name, operands, in_specs, out_shape, out_specs=None, scratch=(), micros=1, limit=24, **more):
    return pl.pallas_call(
        kernel,
        in_specs=in_specs,
        out_specs=[VMEM] * len(out_shape) if out_specs is None else out_specs,
        out_shape=out_shape,
        scratch_shapes=list(scratch),
        compiler_params=pltpu.CompilerParams(vmem_limit_bytes=limit * 2**20),
        cost_estimate=pl.CostEstimate(flops=int(micros * 9e8), bytes_accessed=1, transcendentals=0),
        name=name,
        **more,
    )(*operands)


def whole(array):
    return pl.BlockSpec(array.shape, lambda i: (0,) * array.ndim)


def dot_nt(left, right):
    return lax.dot_general(left, right, (((1,), (1,)), ((), ())), preferred_element_type=FULL)


def dot_tn(left, right):
    return lax.dot_general(left, right, (((0,), (0,)), ((), ())), preferred_element_type=FULL)


def round_ring(value, steps):
    count = lax.axis_size("seq")
    return lax.ppermute(value, "seq", [(i, (i + steps) % count) for i in range(count)])


def swapped(value, axis, stride):
    count = lax.axis_size(axis)
    return lax.ppermute(value, axis, [(i, i ^ stride) for i in range(count)])


def pack_kernel(k_ref, v_ref, grad_ref, pre_ref, up_hbm, down_hbm, up_ref, down_ref, in_sems, out_sems):
    frames, cols = k_ref.shape
    arriving, leaving = [], []
    for out_hbm, out_ref, start, edge in (
        (up_hbm, up_ref, frames - WIN, frames - EDGE), (down_hbm, down_ref, 0, 0)
    ):
        for source, rows, count, first, span in (
            (k_ref, 0, WIN, start, slice(0, cols)),
            (v_ref, 0, WIN, start, slice(cols, 2 * cols)),
            (grad_ref, WIN, EDGE, edge, slice(0, 2 * cols)),
            (pre_ref, WIN + EDGE, EDGE, edge, slice(0, cols)),
            (pre_ref, WIN + EDGE, EDGE, edge, slice(cols, 2 * cols)),
        ):
            i = len(arriving)
            target = out_ref.at[pl.ds(rows, count), span]
            arriving.append(pltpu.make_async_copy(source.at[pl.ds(first, count)], target, in_sems.at[i]))
            leaving.append(pltpu.make_async_copy(target, out_hbm.at[pl.ds(rows, count), span], out_sems.at[i]))
    for copy in arriving:
        copy.start()
    for before, after in zip(arriving, leaving):
        before.wait()
        after.start()
    for copy in leaving:
        copy.wait()


def pack(k_rows, v_rows, out_rows, pre_rows):
    dims = (WIN + 2 * EDGE, 2 * k_rows.shape[1])
    return call(
        pack_kernel, "pack", (k_rows, v_rows, out_rows, pre_rows), [HBM] * 4, [shape(dims)] * 2,
        out_specs=[HBM] * 2,
        scratch=[pltpu.VMEM(dims, LOW)] * 2 + [pltpu.SemaphoreType.DMA((10,))] * 2, limit=58,
    )


def pre_grad(out_rows, pre_rows, proj):
    pre = pre_rows.astype(FULL)
    logistic = jax.nn.sigmoid(pre)
    slope = logistic * (1.0 + pre * (1.0 - logistic))
    return (dot_nt(out_rows, proj) * slope).astype(LOW), (pre * logistic).astype(LOW)


def conv_strip(rows, taps):
    count = rows.shape[0] - 2 * EDGE
    total = jnp.zeros((count, rows.shape[1]), FULL)
    for shift in range(8):
        moved = rows[shift : shift + count + 24]
        for coarse in range(4):
            step = 8 * coarse + shift
            if step >= 1:
                total = total + taps[TAPS - step : TAPS - step + 1] * moved[8 * coarse : 8 * coarse + count]
    return total


def glu_grads(grad_conv, logistic, value):
    first = grad_conv * logistic
    return first.astype(LOW), (first * value * (1.0 - logistic)).astype(LOW)


def front_kernel(
    place, out_ref, pre_ref, proj_ref, input_ref, glu_w_ref, taps_ref,
    mid_ref, glu_ref, act_ref, rim_ref, rim_gate_ref, rim_value_ref,
    padded, taps, gates, values,
):
    frames, cols = pre_ref.shape
    first, length = place[0], place[1]
    inner = frames - EDGE
    taps[:TAPS] = taps_ref[...].astype(FULL)
    for part in range(0, cols, 256):
        span = slice(part, part + 256)
        grad_act = dot_nt(out_ref[...], proj_ref[span])
        for at in range(0, frames, 64):
            rows = slice(at, at + 64)
            pre = pre_ref[rows, span].astype(FULL)
            logistic = jax.nn.sigmoid(pre)
            slope = logistic * (1.0 + pre * (1.0 - logistic))
            padded[rows, span] = (grad_act[rows] * slope).astype(LOW).astype(FULL)
            act_ref[rows, span] = (pre * logistic).astype(LOW)
        rim_ref[: 2 * EDGE, span] = padded[: 2 * EDGE, span].astype(LOW)
        rim_ref[2 * EDGE :, span] = padded[frames - 2 * EDGE :, span].astype(LOW)
        values[:, span] = jnp.dot(input_ref[...], glu_w_ref[0, :, span], preferred_element_type=FULL)
        gate_half = jnp.dot(input_ref[...], glu_w_ref[1, :, span], preferred_element_type=FULL)
        for at in range(0, frames, 64):
            gates[at : at + 64, span] = jax.nn.sigmoid(gate_half[at : at + 64])
    for whole, rim in ((gates, rim_gate_ref), (values, rim_value_ref)):
        rim[:EDGE] = whole[:EDGE]
        rim[EDGE:] = whole[inner:]

    def strip(i, carry):
        at = pl.multiple_of(i * STRIP, STRIP)
        rows = pl.ds(pl.multiple_of(at + EDGE, EDGE), STRIP)
        frame = lax.broadcasted_iota(jnp.int32, (STRIP, 128), 0) + (first + EDGE + at)
        valid = frame < length
        for part in range(0, cols, 128):
            span = slice(part, part + 128)
            grad_conv = conv_strip(padded[pl.ds(at, STRIP + 2 * EDGE), span], taps[:, span])
            grad_conv = jnp.where(valid, grad_conv, 0.0)
            low = glu_grads(grad_conv, gates[rows, span], values[rows, span])
            glu_ref[rows, span] = low[0]
            glu_ref[rows, cols + part : cols + part + 128] = low[1]
        return carry

    lax.fori_loop(0, (frames - 2 * EDGE) // STRIP, strip, 0)
    for part in range(0, mid_ref.shape[1], 256):
        span = slice(part, part + 256)
        mid_ref[:, span] = (
            dot_nt(glu_ref[EDGE:inner, :cols], glu_w_ref[0, span])
            + dot_nt(glu_ref[EDGE:inner, cols:], glu_w_ref[1, span])
        ).astype(LOW)


def front(place, out_rows, pre_rows, proj, input_rows, glu_weight, taps):
    frames, cols = pre_rows.shape
    wide = input_rows.shape[1]
    return call(
        front_kernel, "front",
        (place, out_rows, pre_rows, proj, input_rows, glu_weight, taps),
        [SMEM] + [VMEM] * 6,
        [
            shape((frames - 2 * EDGE, wide)), shape((frames, 2 * cols)), shape((frames, cols)),
            shape((4 * EDGE, cols)), shape((2 * EDGE, cols), FULL), shape((2 * EDGE, cols), FULL),
        ],
        scratch=[
            pltpu.VMEM((frames, cols), FULL), pltpu.VMEM((32, cols), FULL),
            pltpu.VMEM((frames, cols), FULL), pltpu.VMEM((frames, cols), FULL),
        ],
        micros=7,
    )


def rim_kernel(
    place, before_ref, after_ref, rim_ref, gate_ref, value_ref, proj_ref, glu_w_ref, taps_ref, glu_in_ref,
    part_ref, glu_ref,
):
    frames = glu_ref.shape[0]
    cols = rim_ref.shape[1]
    first, length, total = place[0], place[1], place[2]
    del glu_in_ref
    out_rows = jnp.concatenate([before_ref[:EDGE], after_ref[:EDGE]], axis=0)
    pre_rows = jnp.concatenate([before_ref[EDGE:, :cols], after_ref[EDGE:, :cols]], axis=0)
    arrived = pre_grad(out_rows, pre_rows, proj_ref[...])[0].astype(FULL)
    above = jnp.where(first > 0, arrived[:EDGE], 0.0)
    below = jnp.where(first + frames < total, arrived[EDGE:], 0.0)
    own = rim_ref[...].astype(FULL)
    taps = taps_ref[...].astype(FULL)
    pieces = []
    for rows, start, place_of in (
        (jnp.concatenate([above, own[: 2 * EDGE]], axis=0), 0, slice(0, EDGE)),
        (jnp.concatenate([own[2 * EDGE :], below], axis=0), frames - EDGE, slice(EDGE, 2 * EDGE)),
    ):
        lows = []
        for part in range(0, cols, 128):
            span = slice(part, part + 128)
            frame = lax.broadcasted_iota(jnp.int32, (EDGE, 128), 0) + (first + start)
            grad_conv = jnp.where(frame < length, conv_strip(rows[:, span], taps[:, span]), 0.0)
            lows.append(glu_grads(grad_conv, gate_ref[place_of, span], value_ref[place_of, span]))
        low = jnp.concatenate([pair[0] for pair in lows] + [pair[1] for pair in lows], axis=1)
        glu_ref[start : start + EDGE] = low
        pieces.append(low)
    low = jnp.concatenate(pieces, axis=0)
    part_ref[...] = (dot_nt(low[:, :cols], glu_w_ref[0]) + dot_nt(low[:, cols:], glu_w_ref[1])).astype(LOW)


def rim(place, before, after, rim_rows, gate, value, proj, glu_weight, taps, glu_low):
    edge = pl.BlockSpec((2 * EDGE, before.shape[1]), lambda i: (WIN // (2 * EDGE), 0))
    wide = glu_weight.shape[1]
    return call(
        rim_kernel, "rim",
        (place, before, after, rim_rows, gate, value, proj, glu_weight, taps, glu_low),
        [SMEM, edge, edge, whole(rim_rows), whole(gate), whole(value), VMEM, VMEM, whole(taps), VMEM],
        [shape((2 * EDGE, wide)), shape(glu_low.shape)],
        out_specs=[pl.BlockSpec((2 * EDGE, wide), lambda i: (0, 0)), VMEM],
        grid=(1,), micros=0.1, input_output_aliases={9: 1},
    )


def terms_kernel(keeps, place, input_ref, glu_ref, out_ref, act_ref, *refs):
    core = place[3]
    cols = act_ref.shape[1]
    rows = input_ref.shape[1] // 4
    peers = 8
    share = rows // peers
    sources = ((input_ref, glu_ref, 0), (input_ref, glu_ref, cols), (out_ref, act_ref, 0))
    leaving = []
    for which, (source, low, start) in enumerate(sources):
        for half in range(2):
            block = 2 * half + (core if keeps else 1 - core)
            left = source[:, pl.ds(pl.multiple_of(block * rows, rows), rows)]
            for part in range(0, cols, 256):
                term = dot_tn(left, low[:, start + part : start + part + 256])
                at = slice(part, part + 256)
                if not keeps:
                    refs[which][half, :, at] = term.astype(LOW)
                    continue
                term = term + refs[which][half, :, at].astype(FULL)
                at = slice(cols * which + part, cols * which + part + 256)
                for peer, moved in enumerate(by_peer(term, peers)):
                    refs[4][peer, half * share : (half + 1) * share, at] = moved.astype(LOW)
        if keeps:
            at = slice(cols * which, cols * which + cols)
            leaving.append(pltpu.make_async_copy(refs[4].at[:, :, at], refs[3].at[:, :, at], refs[5].at[which]))
            leaving[-1].start()
    for copy in leaving:
        copy.wait()


def terms(place, input_rows, glu_low, out_rows, activated, arrived=()):
    wide, cols = input_rows.shape[1], activated.shape[1]
    operands = (place, input_rows, glu_low, out_rows, activated) + tuple(arrived)
    joined = (8, wide // 16, 3 * cols)
    if arrived:
        more = dict(out_specs=[HBM], scratch=[pltpu.VMEM(joined, LOW), pltpu.SemaphoreType.DMA((3,))])
    else:
        more = {}
    return call(
        functools.partial(terms_kernel, bool(arrived)), "terms",
        operands, [SMEM] + [VMEM] * (len(operands) - 1),
        [shape(joined)] if arrived else [shape((2, wide // 4, cols))] * 3, micros=0.1, **more,
    )


def resid_kernel(
    place, out_ref, mid_ref, far_mid_ref, part_ref, far_part_ref, weight_ref, attended_ref,
    resid_ref, grad_ref, send_ref, keep_ref,
):
    frames = out_ref.shape[0]
    first, length, core = place[0], place[1], place[3]
    inner = frames - EDGE

    def total(rows, own, far):
        resid_ref[rows] = (out_ref[rows].astype(FULL) + (own.astype(FULL) + far.astype(FULL))).astype(LOW)

    total(slice(0, EDGE), part_ref[:EDGE], far_part_ref[:EDGE])
    total(slice(EDGE, inner), mid_ref[...], far_mid_ref[...])
    total(slice(inner, frames), part_ref[EDGE:], far_part_ref[EDGE:])
    rows = send_ref.shape[1]
    for out, flip in ((send_ref, 1), (keep_ref, 0)):
        for half in range(2):
            block = 2 * half + (1 - core if flip else core)
            span = pl.ds(pl.multiple_of(block * rows, rows), rows)
            out[half] = dot_tn(resid_ref[:, span], attended_ref[...]).astype(LOW)
    frame = lax.broadcasted_iota(jnp.int32, grad_ref.shape, 0) + first
    grad = dot_nt(resid_ref[...], weight_ref[...])
    grad_ref[...] = jnp.where(frame < length, grad, 0.0).astype(LOW)


def resid(place, out_rows, mid, far_mid, part, far_part, weight, attended):
    frames, wide = out_rows.shape
    cols = attended.shape[1]
    return call(
        resid_kernel, "resid",
        (place, out_rows, mid, far_mid, part, far_part, weight, attended),
        [SMEM] + [VMEM] * 7,
        [shape((frames, wide)), shape((frames, cols))] + [shape((2, wide // 4, cols))] * 2, micros=60,
    )


def by_peer(rows, peers):
    groups = rows.reshape(rows.shape[0] // (8 * peers), peers, 8, rows.shape[1])
    return [groups[:, peer].reshape(-1, rows.shape[1]) for peer in range(peers)]


def add_kernel(own_ref, arrived_ref, sum_ref):
    peers, share = sum_ref.shape[0], sum_ref.shape[1] // 2
    for half in range(2):
        total = own_ref[half].astype(FULL) + arrived_ref[half].astype(FULL)
        for peer, rows in enumerate(by_peer(total, peers)):
            sum_ref[peer, half * share : (half + 1) * share] = rows.astype(LOW)


def add(own, arrived, peers):
    halves, rows, cols = own.shape
    dims = (peers, halves * rows // peers, cols)
    return call(add_kernel, "add", (own, arrived), [VMEM, VMEM], [shape(dims)])[0]


def plane_kernel(*refs):
    *sources, sum_ref = refs
    at = 0
    for parts_ref in sources:
        if parts_ref.ndim == 2:
            at = parts_ref.shape[1]
            sum_ref[:, :at] = parts_ref[...]
            continue
        for start in range(0, parts_ref.shape[2], 256):
            lanes = slice(start, start + 256)
            total = parts_ref[0, :, lanes].astype(FULL)
            for i in range(1, parts_ref.shape[0]):
                total = total + parts_ref[i, :, lanes].astype(FULL)
            sum_ref[:, at : at + 256] = total.astype(LOW)
            at += 256


def plane_sum(*parts):
    dims = (parts[0].shape[-2], sum(part.shape[-1] for part in parts))
    return call(plane_kernel, "plane_sum", parts, [VMEM] * len(parts), [shape(dims)])[0]


def line_kernel(parts_ref, out_ref, glu_ref, proj_ref):
    total = parts_ref[0].astype(FULL)
    for i in range(1, parts_ref.shape[0]):
        total = total + parts_ref[i].astype(FULL)
    cols = out_ref.shape[1]
    glu_ref[0] = total[:, :cols].astype(LOW)
    glu_ref[1] = total[:, cols : 2 * cols].astype(LOW)
    proj_ref[...] = total[:, 2 * cols : 3 * cols].astype(LOW)
    out_ref[...] = total[:, 3 * cols :].astype(LOW)


def line_sum(parts):
    rows, cols = parts.shape[1], parts.shape[2] // 4
    return call(
        line_kernel, "line_sum", (parts,), [VMEM], [shape((rows, cols)), shape((2, rows, cols)), shape((rows, cols))]
    )


def exchanged(parts, groups):
    return lax.all_to_all(parts, ("dp", "seq"), 0, 0, axis_index_groups=groups)


BLOCK = 128
CHUNK = 128
SPAN = BLOCK + 2 * WIN
SCALE = HEAD_DIM**-0.5
PAIR = 2 * HEAD_DIM


def side_by_side(rows):
    lane = lax.broadcasted_iota(jnp.int32, rows.shape, 1)
    zero = jnp.zeros_like(rows)
    return jnp.concatenate(
        [jnp.where(lane < HEAD_DIM, rows, zero), jnp.where(lane < HEAD_DIM, zero, rows)], axis=0
    )


def own_columns(columns):
    return jnp.concatenate([columns[:HEAD_DIM, :BLOCK], columns[HEAD_DIM:, BLOCK:]], axis=0)


def gather_rows(whole, before_ref, own_ref, after_ref):
    frames = own_ref.shape[0]
    whole[:WIN] = before_ref[...]
    whole[WIN : WIN + frames] = own_ref[...]
    whole[WIN + frames :] = after_ref[...]


def pair_specs(frames, pairs, start=0):
    own = pl.BlockSpec((frames, PAIR), lambda i: (0, i + start))
    far_key = pl.BlockSpec((WIN, PAIR), lambda i: (0, i + start))
    far_value = pl.BlockSpec((WIN, PAIR), lambda i: (0, i + start + pairs))
    return own, far_key, far_value


def attend_kernel(
    place, q_ref, k_ref, v_ref, kb_ref, vb_ref, ka_ref, va_ref,
    weight_ref, out_ref, share_ref, fill, scores, keys, values,
):
    first, length = place[0], place[1]
    frames = q_ref.shape[0]

    @pl.when(pl.program_id(0) == 0)
    def _():
        for block in range(frames // BLOCK):
            key = lax.broadcasted_iota(jnp.int32, (SPAN, BLOCK), 0)
            offset = key - lax.broadcasted_iota(jnp.int32, (SPAN, BLOCK), 1)
            frame = key + (first - WIN + block * BLOCK)
            allowed = (offset >= 0) & (offset <= 2 * WIN) & (frame >= 0) & (frame < length)
            fill[block] = jnp.where(allowed, 0.0, NEG_FILL)

    gather_rows(keys, kb_ref, k_ref, ka_ref)
    gather_rows(values, vb_ref, v_ref, va_ref)
    for block in range(frames // BLOCK):
        rows = slice(block * BLOCK, (block + 1) * BLOCK)
        start = block * BLOCK
        queries = side_by_side(q_ref[rows] * SCALE)
        top = jnp.full((8, 2 * BLOCK), NEG_FILL, FULL)
        for at in range(0, SPAN, CHUNK):
            part = dot_nt(keys[start + at : start + at + CHUNK], queries)
            bias = fill[block, at : at + CHUNK]
            part = part + jnp.concatenate([bias, bias], axis=1)
            scores[at : at + CHUNK] = part
            top = jnp.maximum(top, jnp.max(part.reshape(CHUNK // 8, 8, 2 * BLOCK), axis=0))
        top = jnp.max(top, axis=0, keepdims=True)
        total = jnp.zeros((8, 2 * BLOCK), FULL)
        for at in range(0, SPAN, CHUNK):
            part = jnp.exp(scores[at : at + CHUNK] - top)
            total = total + jnp.sum(part.reshape(CHUNK // 8, 8, 2 * BLOCK), axis=0)
            weight_ref[0, block, at : at + CHUNK] = part.astype(LOW)
        share = 1.0 / jnp.sum(total, axis=0, keepdims=True)
        summed = own_columns(dot_tn(values[start : start + SPAN], weight_ref[0, block]) * share)
        frame = lax.broadcasted_iota(jnp.int32, (1, BLOCK), 1) + (first + block * BLOCK)
        out_ref[rows] = jnp.where(frame < length, summed, 0.0).T.astype(LOW)
        share_ref[rows] = own_columns(jnp.broadcast_to(share, (PAIR, 2 * BLOCK))).T


def attend_grad_kernel(
    q_ref, k_ref, v_ref, kb_ref, vb_ref, ka_ref, va_ref, weight_ref, out_ref, share_ref, grad_ref, *refs
):
    dq_ref, dk_ref, dv_ref, to_before_ref, to_after_ref, keys, values, key_sum, value_sum = refs[-9:]
    frames = q_ref.shape[0]
    gather_rows(keys, kb_ref, k_ref, ka_ref)
    gather_rows(values, vb_ref, v_ref, va_ref)
    key_sum[...] = jnp.zeros_like(key_sum)
    value_sum[...] = jnp.zeros_like(value_sum)
    for block in range(frames // BLOCK):
        rows = slice(block * BLOCK, (block + 1) * BLOCK)
        span = slice(block * BLOCK, block * BLOCK + SPAN)
        queries = side_by_side(q_ref[rows] * SCALE)
        grad_rows = (grad_ref[rows].astype(FULL) * share_ref[rows]).astype(LOW)
        grads = side_by_side(grad_rows)
        product = (grad_rows.astype(FULL) * out_ref[rows].astype(FULL)).T
        row_delta = jnp.concatenate(
            [
                jnp.sum(product[:HEAD_DIM], axis=0, keepdims=True),
                jnp.sum(product[HEAD_DIM:], axis=0, keepdims=True),
            ],
            axis=1,
        )
        weight = weight_ref[0, block]
        grad_prob = dot_nt(values[span], grads)
        grad_score = (weight.astype(FULL) * (grad_prob - row_delta)).astype(LOW)
        value_sum[span] += jnp.dot(weight, grads, preferred_element_type=FULL)
        key_sum[span] += jnp.dot(grad_score, queries, preferred_element_type=FULL)
        grad_query = dot_tn(keys[span], grad_score)
        dq_ref[rows] = (own_columns(grad_query).T * SCALE).astype(LOW)
    for total, inner, lane in ((key_sum, dk_ref, 0), (value_sum, dv_ref, PAIR)):
        to_before_ref[:, lane : lane + PAIR] = total[:WIN].astype(LOW)
        inner[...] = total[WIN : WIN + frames]
        to_after_ref[:, lane : lane + PAIR] = total[WIN + frames :].astype(LOW)


def attend(place, q_rows, k_rows, v_rows, before, after):
    frames, cols = q_rows.shape
    pairs, blocks = cols // PAIR, frames // BLOCK
    own, far_key, far_value = pair_specs(frames, pairs)
    return call(
        attend_kernel, "attend", (place, q_rows, k_rows, v_rows, before, before, after, after),
        [SMEM, own, own, own, far_key, far_value, far_key, far_value],
        [shape((pairs, blocks, SPAN, 2 * BLOCK)), shape((frames, cols)), shape((frames, cols), FULL)],
        out_specs=[pl.BlockSpec((1, blocks, SPAN, 2 * BLOCK), lambda i: (i, 0, 0, 0)), own, own],
        scratch=[pltpu.VMEM((blocks, SPAN, BLOCK), FULL), pltpu.VMEM((SPAN, 2 * BLOCK), FULL)] + [pltpu.VMEM((frames + 2 * WIN, PAIR), LOW)] * 2,
        grid=(pairs,), micros=0.5, limit=57,
    )


def attend_grad(q_rows, k_rows, v_rows, before, after, weight, attended, share, grad_attn, start, count, earlier=()):
    frames, cols = q_rows.shape
    pairs, blocks = cols // PAIR, frames // BLOCK
    own, far_key, far_value = pair_specs(frames, pairs, start)
    far = pl.BlockSpec((WIN, 2 * PAIR), lambda i: (0, i + start))
    weights = pl.BlockSpec((1, blocks, SPAN, 2 * BLOCK), lambda i: (i + start, 0, 0, 0))
    return call(
        attend_grad_kernel, "attend_grad",
        (q_rows, k_rows, v_rows, before, before, after, after, weight, attended, share, grad_attn, *earlier),
        [own, own, own, far_key, far_value, far_key, far_value, weights, own, own, own] + [HBM] * len(earlier),
        [shape((frames, cols))] + [shape((frames, cols), FULL)] * 2 + [shape((WIN, 2 * cols))] * 2,
        out_specs=[own, own, own, far, far],
        scratch=[pltpu.VMEM((frames + 2 * WIN, PAIR), LOW)] * 2 + [pltpu.VMEM((frames + 2 * WIN, PAIR), FULL)] * 2,
        grid=(count,), micros=1, limit=58,
        input_output_aliases={11 + i: i for i in range(len(earlier))},
    )


def finish_kernel(dk_ref, dv_ref, from_before_ref, from_after_ref, key_ref, value_ref):
    frames, cols = dk_ref.shape
    shared = frames - WIN
    for own, out, lane in ((dk_ref, key_ref, 0), (dv_ref, value_ref, PAIR)):
        for start in range(0, cols, PAIR):
            span = slice(start, start + PAIR)
            far_span = slice(2 * start + lane, 2 * start + lane + PAIR)
            above = own[:WIN, span] + from_before_ref[:, far_span].astype(FULL)
            far = from_after_ref[:, far_span].astype(FULL)
            out[:shared, span] = above[:shared].astype(LOW)
            out[shared:WIN, span] = (above[shared:] + far[: WIN - shared]).astype(LOW)
            out[WIN:, span] = (own[WIN:, span] + far[WIN - shared :]).astype(LOW)


def finish(grad_key, grad_value, from_before, from_after):
    steps = 2
    own = pl.BlockSpec((grad_key.shape[0], grad_key.shape[1] // steps), lambda i: (0, i))
    far = pl.BlockSpec((from_before.shape[0], from_before.shape[1] // steps), lambda i: (0, i))
    return call(
        finish_kernel, "finish", (grad_key, grad_value, from_before, from_after), [own, own, far, far],
        [shape(grad_key.shape)] * 2, out_specs=[own, own], grid=(steps,), micros=2, limit=50,
    )


def local(
    lengths,
    query_act,
    key_act,
    value_act,
    conv_input,
    conv_result,
    out_grad,
    out_weight,
    glu_weight,
    conv_taps,
    proj_weight,
):
    q_rows, k_rows, v_rows = (query_act[0], key_act[0], value_act[0])
    input_rows, pre_rows, out_rows = (conv_input[0], conv_result[0], out_grad[0])
    frames, cols = q_rows.shape
    peers = lax.axis_size("seq")
    index = lax.axis_index("dp")
    first = lax.axis_index("seq") * frames
    place = jnp.stack([first, lengths[0], peers * frames, index % 2, index // 2]).astype(jnp.int32)

    up, down = pack(k_rows, v_rows, out_rows, pre_rows)
    before, after = (round_ring(up, 1), round_ring(down, -1))
    mid, glu_low, activated, rim_rows, rim_gate, rim_value = front(
        place, out_rows, pre_rows, proj_weight, input_rows, glu_weight, conv_taps
    )
    far_mid = swapped(mid, "tensor", 1)
    part, glu_low = rim(
        place, before, after, rim_rows, rim_gate, rim_value, proj_weight, glu_weight, conv_taps, glu_low
    )
    far_part = swapped(part, "tensor", 1)
    given = [swapped(term, "dp", 1) for term in terms(place, input_rows, glu_low, out_rows, activated)]
    on_chip = terms(place, input_rows, glu_low, out_rows, activated, given)[0]
    q_late, on_chip = lax.optimization_barrier((q_rows, on_chip))
    weight, attended, share = attend(place, q_late, k_rows, v_rows, before, after)
    resid_low, grad_attn, out_send, out_keep = resid(
        place, out_rows, mid, far_mid, part, far_part, out_weight, attended
    )
    near, far = (8, peers // 8)
    by_plane = [[d * peers + z * near + i for i in range(near)] for d in range(4) for z in range(far)]
    by_line = [
        [(2 * y + core) * peers + z * near + i for y in range(2) for z in range(far)]
        for core in range(2) for i in range(near)
    ]
    rest = exchanged(on_chip, by_plane)
    operands = (q_rows, k_rows, v_rows, before, after, weight, attended, share, grad_attn)
    early = attend_grad(*operands, 0, 2)
    out_given, early = lax.optimization_barrier((swapped(out_send, "dp", 1), early))
    on_chip_out = add(out_keep, out_given, near)
    grad_query, grad_key, grad_value, to_before, to_after = attend_grad(*operands, 2, 2, early)
    from_after, from_before = (round_ring(to_before, -1), round_ring(to_after, 1))
    on_chip_out, rest = lax.optimization_barrier((on_chip_out, rest))
    plane = plane_sum(plane_sum(rest), exchanged(on_chip_out, by_plane))
    out_sum, glu_sum, proj_sum = line_sum(exchanged(plane.reshape(2 * far, -1, plane.shape[1]), by_line))
    key_grad, value_grad = finish(grad_key, grad_value, from_before, from_after)
    return (
        resid_low[None],
        grad_query[None],
        key_grad[None],
        value_grad[None],
        out_sum.T,
        glu_sum,
        proj_sum.T,
    )


def solution(mesh):
    in_specs = (
        P("dp"),
        P("dp", "seq", "tensor"),
        P("dp", "seq", "tensor"),
        P("dp", "seq", "tensor"),
        P("dp", "seq", None),
        P("dp", "seq", "tensor"),
        P("dp", "seq", None),
        P("tensor", None),
        P(None, None, "tensor"),
        P(None, "tensor"),
        P("tensor", None),
    )
    out_specs = (
        P("dp", "seq", None),
        P("dp", "seq", "tensor"),
        P("dp", "seq", "tensor"),
        P("dp", "seq", "tensor"),
        P("tensor", ("dp", "seq")),
        P(None, ("dp", "seq"), "tensor"),
        P("tensor", ("dp", "seq")),
    )
    return jax.shard_map(local, mesh=mesh, in_specs=in_specs, out_specs=out_specs, check_vma=False)
```
